512 devices in a mesh: scen: 64 (over x, z), per: 8 (over y, core).
Axes of the slice: x: 4, y: 4, z: 16, core: 2. Of those that a mesh axis runs over, the one named last changes fastest.
Arguments:
- dual_start: float32 [512, 16, 8192], P('scen', 'per'), may hold values from -6 to 6
- demand: float32 [512, 16, 8192], P('scen', 'per'), may hold values from -6 to 6
- cost: float32 [16, 8192], P('per'), may hold values from -6 to 6
- upper: float32 [16, 8192], P('per'), may hold values from 0.2 to 1
- carry: float32 [16, 8192], P('per'), may hold values from 0.3 to 1
- prob: float32 [512], P('scen'), may hold values from 1 to 10
- section_size: int32 [16], P('per'), may hold values from 1 to 512, as said below
- block_cols: int32 [16, 16, 3], P('per'), may hold values from 0 to 15, as said below
- block_pool: int32 [16, 16, 3], P('per'), may hold values from 0 to 2
- pool_tiles: float32 [3, 512, 512], replicated, may hold values from -0.15625 to 0.15625
- step_table: float32 [4, 2], replicated, may hold values from 0.1 to 0.4
- subtree_step: int32 [8], replicated, may hold values from 0 to 3
- restart: int32 [2, 16], P(None, 'per'), may hold values 0 or 1
Outputs:
- primal: float32 [512, 16, 8192], P('scen', 'per')
- dual: float32 [512, 16, 8192], P('scen', 'per')
The draws below stay inside these ranges and needn't reach their ends.
Inputs may be any that keep to these rules, and one draw needn't show every extreme that they name: `section_size`: each value is a power of two that divides the one before it; the first period's is 512 and the last period's is 1. `block_cols`: the 3 column blocks named for one block row of one period differ.
All inputs are finite; a program needn't handle non-finite values. No bound on the sum of `restart` on one device may be relied on, other than what follows from the above.
Results may differ from the reference program's by a relative error of at most 0.0001.
Values sent between devices are 32-bit elements; how exact they have to be, the bound alone decides.
No kernel may reach another device: no remote copies, remote signals or barrier semaphores. Data moves between devices by JAX's collectives and lax.ppermute only.
A program may use at most 64 MiB of HBM per device.

```python
import math
import jax
import jax.numpy as jnp
from jax import lax

R = 8192
TILE = 512
NB = 3
NPOOL = 3
ITERS = 2
SUBTREES = 8
NSTEP = 4
RB = 16
SCEN = 512
PERIODS = 16


def draw_section_size(key, part):
    key = jax.random.fold_in(key, 11)
    levels = int(SCEN).bit_length() - 1
    moment = jax.random.randint(key, (levels,), 0, PERIODS - 1)
    period = jnp.arange(PERIODS, dtype=jnp.int32)
    passed = jnp.sum((moment[None, :] < period[:, None]).astype(jnp.int32), axis=1)
    return (SCEN // 2 ** passed).astype(jnp.int32)


def pick_columns(one_key):
    return jax.random.permutation(one_key, RB)[:NB]


def draw_block_cols(key, part):
    key = jax.random.fold_in(key, 12)
    several = jax.random.split(key, PERIODS * RB)
    picked = jax.vmap(pick_columns)(several)
    return picked.reshape(PERIODS, RB, NB).astype(jnp.int32)


def touch_ends(array, rng, least, largest):
    longest = array.shape.index(max(array.shape))
    spots = []
    for shift in (0, 1):
        where = [jax.random.randint(jax.random.fold_in(rng, axis), (), 0, length) for axis, length in enumerate(array.shape)]
        where[longest] = (where[longest] + shift) % array.shape[longest]
        spots.append(tuple(where))
    return array.at[spots[0]].set(least).at[spots[1]].set(largest)


def steps_of(stream_key, dims, pieces, least, high):
    factor_of, own = 1.0, jax.random.fold_in(stream_key, 6)
    for dim, blocks in pieces:
        draws = jnp.exp(jax.random.uniform(jax.random.fold_in(own, dim), (blocks,), jnp.float32, least / len(pieces), high / len(pieces)))
        factor_of = factor_of * jnp.repeat(draws, dims[dim] // blocks).reshape([-1 if axis == dim else 1 for axis in range(len(dims))])
    return factor_of


def gaussian(key, extent, deviation, limit, cuts=(), kind=jnp.bfloat16):
    loudness = steps_of(key, extent, cuts, -0.22, 0.18) if cuts else 1.0
    drawn = jax.random.normal(key, extent, jnp.float32) * deviation * loudness
    return jnp.minimum(jnp.maximum(drawn, -limit), limit).astype(kind)


def setup_inputs(seed: int = 0) -> dict:
    streams_of = jax.random.split(jax.random.key(seed), 14)
    dual_start = gaussian(streams_of[0], (SCEN, PERIODS, R), 1.0, 6.0, ((0, 64), (1, 8)), jnp.float32)
    demand = gaussian(streams_of[1], (SCEN, PERIODS, R), 1.0, 6.0, ((0, 64), (1, 8)), jnp.float32)
    cost = gaussian(streams_of[2], (PERIODS, R), 1.0, 6.0, ((0, 8),), jnp.float32)
    upper = jnp.clip(0.2 + 0.8 * jax.random.uniform(streams_of[3], (PERIODS, R), jnp.float32) ** steps_of(streams_of[3], (PERIODS, R), ((0, 8),), -0.2, 0.2), 0.2, 1.0)
    carry = jnp.clip(0.3 + 0.7 * jax.random.uniform(streams_of[4], (PERIODS, R), jnp.float32) ** steps_of(streams_of[4], (PERIODS, R), ((0, 8),), -0.2, 0.2), 0.3, 1.0)
    prob = jnp.clip(jnp.exp(math.log(10.0) - 2.3025851 * jax.random.uniform(streams_of[5], (SCEN,), jnp.float32) ** steps_of(streams_of[5], (SCEN,), ((0, 64),), -0.2, 0.2)), 1.0, 10.0)
    section_size = draw_section_size(jax.random.fold_in(streams_of[13], 71), 0)
    block_cols = draw_block_cols(jax.random.fold_in(streams_of[13], 71), 0)
    block_pool = touch_ends(jax.random.randint(streams_of[8], (PERIODS, RB, NB), 0, NPOOL), jax.random.fold_in(streams_of[8], 1), 0, NPOOL - 1).astype(jnp.int32)
    pool_tiles = gaussian(streams_of[9], (NPOOL, TILE, TILE), (NB * TILE) ** -0.5, 0.15625, (), jnp.float32)
    step_table = jnp.clip(jnp.exp(jax.random.uniform(streams_of[10], (NSTEP, 2), jnp.float32, math.log(0.1), math.log(0.4))), 0.1, 0.4)
    subtree_step = touch_ends(jax.random.randint(streams_of[11], (SUBTREES,), 0, NSTEP), jax.random.fold_in(streams_of[11], 1), 0, NSTEP - 1).astype(jnp.int32)
    restart = touch_ends((jax.random.randint(streams_of[12], (ITERS, PERIODS), 0, 2) < 1).astype(jnp.int32), jax.random.fold_in(streams_of[12], 1), 0, 1)
    return {"dual_start": dual_start, "demand": demand, "cost": cost, "upper": upper, "carry": carry, "prob": prob, "section_size": section_size, "block_cols": block_cols, "block_pool": block_pool, "pool_tiles": pool_tiles, "step_table": step_table, "subtree_step": subtree_step, "restart": restart}


HIGHEST = lax.Precision.HIGHEST


def selection(block_cols, block_pool):
    labels = block_pool * RB + block_cols
    labels_all = jnp.arange(NPOOL * RB, dtype=jnp.int32)
    counted = jnp.sum((labels[..., None] == labels_all).astype(jnp.float32), axis=2)
    return counted.reshape(counted.shape[0], RB, NPOOL, RB)


def apply_blocks(fields, select, pool_tiles):
    scenarios, periods, feature = fields.shape
    blocks = fields.reshape(scenarios, periods, RB, TILE)
    images = jnp.einsum('spct,jut->spjcu', blocks, pool_tiles, precision=HIGHEST)
    result = jnp.einsum('pijc,spjcu->spiu', select, images, precision=HIGHEST)
    return result.reshape(scenarios, periods, feature)


def apply_blocks_transposed(fields, select, pool_tiles):
    scenarios, periods, feature = fields.shape
    blocks = fields.reshape(scenarios, periods, RB, TILE)
    images = jnp.einsum('spiu,jut->spjit', blocks, pool_tiles, precision=HIGHEST)
    result = jnp.einsum('pijc,spjit->spct', select, images, precision=HIGHEST)
    return result.reshape(scenarios, periods, feature)


def forward(fields, carry, select, pool_tiles):
    previous = jnp.concatenate([jnp.zeros_like(fields[:, :1]), fields[:, :-1]], axis=1)
    return apply_blocks(fields, select, pool_tiles) - carry[None] * previous


def backward(fields, carry, select, pool_tiles):
    carried = carry[None] * fields
    following = jnp.concatenate([carried[:, 1:], jnp.zeros_like(carried[:, :1])], axis=1)
    return apply_blocks_transposed(fields, select, pool_tiles) - following


def tree_average(values, prob, section_size):
    scen_ids = jnp.arange(SCEN, dtype=jnp.int32)
    groups = scen_ids[None, :] // section_size[:, None]
    same_group = (groups[:, :, None] == groups[:, None, :]).astype(jnp.float32)
    weighting = same_group * prob[None, None, :]
    numerator = jnp.einsum('psq,qpr->spr', weighting, values, precision=HIGHEST)
    denominator = jnp.sum(weighting, axis=2)
    return numerator / denominator.T[:, :, None]


def reference(dual_start, demand, cost, upper, carry, prob, section_size, block_cols, block_pool, pool_tiles, step_table, subtree_step, restart):
    scen_ids = jnp.arange(SCEN, dtype=jnp.int32)
    subtree = scen_ids // (SCEN // SUBTREES)
    entry = subtree_step[subtree]
    primal_step = step_table[entry, 0][:, None, None]
    dual_step = step_table[entry, 1][:, None, None]
    select = selection(block_cols, block_pool)
    primal = jnp.zeros((SCEN, PERIODS, R), jnp.float32)
    dual = dual_start
    primal_mean = primal
    dual_mean = dual
    count = jnp.ones((PERIODS,), jnp.float32)
    for iteration in range(ITERS):
        gradient = cost[None] - backward(dual, carry, select, pool_tiles)
        averaged = tree_average(primal - primal_step * gradient, prob, section_size)
        primal_new = jnp.minimum(jnp.maximum(averaged, 0.0), upper[None])
        probe = 2.0 * primal_new - primal
        dual_new = dual + dual_step * (demand - forward(probe, carry, select, pool_tiles))
        weight_old = count[None, :, None]
        primal_mean = (weight_old * primal_mean + primal_new) / (weight_old + 1.0)
        dual_mean = (weight_old * dual_mean + dual_new) / (weight_old + 1.0)
        flagged = restart[iteration] == 1
        primal = jnp.where(flagged[None, :, None], primal_mean, primal_new)
        dual = jnp.where(flagged[None, :, None], dual_mean, dual_new)
        count = jnp.where(flagged, jnp.float32(1.0), count + 1.0)
    return primal, dual
```

```python
import jax
import jax.numpy as jnp
from jax import lax
from jax.sharding import PartitionSpec as P

TILE = 512
NPOOL = 3
SUBTREES = 8
RB = 16
LANES = 128


HIGHEST = lax.Precision.HIGHEST


def shifted(block, axis, distance):
    devices = range(lax.axis_size(axis))
    route = [(i - distance, i) for i in devices if i - distance in devices]
    return lax.ppermute(block, axis, route)


def selection(block_cols, block_pool):
    labels = block_pool * RB + block_cols
    labels_all = jnp.arange(NPOOL * RB, dtype=jnp.int32)
    counted = jnp.sum((labels[..., None] == labels_all).astype(jnp.float32), axis=2)
    return counted.reshape(counted.shape[0], RB, NPOOL, RB)


def apply_blocks(fields, select, pool_tiles):
    periods, rows, feature = fields.shape
    blocks = fields.reshape(periods, rows, RB, TILE)
    images = jnp.einsum("psct,jut->psjcu", blocks, pool_tiles, precision=HIGHEST)
    result = jnp.einsum("pijc,psjcu->psiu", select, images, precision=HIGHEST)
    return result.reshape(periods, rows, feature)


def apply_blocks_transposed(fields, select, pool_tiles):
    periods, rows, feature = fields.shape
    blocks = fields.reshape(periods, rows, RB, TILE)
    images = jnp.einsum("psiu,jut->psjit", blocks, pool_tiles, precision=HIGHEST)
    result = jnp.einsum("pijc,psjit->psct", select, images, precision=HIGHEST)
    return result.reshape(periods, rows, feature)


def local_weights(section, prob):
    rows = prob.shape[0]
    inside = jnp.clip(section, 1, rows)
    group = jnp.arange(rows, dtype=jnp.int32)[None, :] // inside[:, None]
    same = (group[:, :, None] == group[:, None, :]).astype(jnp.float32) * prob[None, None, :]
    return same / jnp.sum(same, axis=2, keepdims=True)


def membership(section, rows, devices):
    span = jnp.maximum(section // rows, 1)
    group = jnp.arange(devices, dtype=jnp.int32)[None, :] // span[:, None]
    return (group[:, :, None] == group[:, None, :]).astype(jnp.float32)


def clipped(values, upper):
    return jnp.minimum(jnp.maximum(values, 0.0), upper)


def mixed(matrix, values):
    return jnp.einsum("pnm,pmr->pnr", matrix, values, precision=HIGHEST)


def per_device(
    dual_start,
    demand,
    cost,
    upper,
    carry,
    prob,
    section_size,
    block_cols,
    block_pool,
    pool_tiles,
    step_table,
    subtree_step,
    restart,
):
    rows, periods, feature = dual_start.shape
    devices = lax.axis_size("scen")
    device = lax.axis_index("scen")
    chunk = feature // devices
    device_ids = jnp.arange(devices, dtype=jnp.int32)
    steps = step_table[subtree_step[device_ids // (devices // SUBTREES)]]
    product_all = steps[:, 0] * steps[:, 1]
    rate, dual_rate = steps[device, 0], steps[device, 1]
    product = rate * dual_rate
    select = selection(block_cols, block_pool)
    damp = jnp.where(restart[0] == 1, 0.5, 1.0).astype(jnp.float32)
    start = dual_start.transpose(1, 0, 2)
    target = demand.transpose(1, 0, 2)
    moved = start + damp[:, None, None] * dual_rate * target
    both = jnp.concatenate([start, moved], axis=1)
    carried = carry[:, None] * both
    arriving = shifted(carried[0], "per", -1)
    square = carry * carry * damp[:, None]
    square_next = jnp.stack([square[1], shifted(square[0], "per", -1)])
    section_before = jnp.stack([shifted(section_size[1], "per", 1), section_size[0]])
    following = jnp.stack([carried[1], arriving])
    raw = rate * (apply_blocks_transposed(both, select, pool_tiles) - following - cost[:, None])
    weights = local_weights(section_size, prob)
    first_local = mixed(weights, raw[:, :rows])
    second_local = mixed(weights, raw[:, rows:])
    new_local = clipped(first_local, upper[:, None])
    mass = jnp.sum(prob)
    wide = (section_size > rows)[:, None]
    pushed = product * jnp.sum(prob[None, :, None] * new_local, axis=1)
    sums = jnp.where(wide, mass * first_local[:, 0], pushed)
    packed = jnp.concatenate(
        [sums, mass * second_local[:, 0], jnp.full((1, feature), 1.0) * mass, jnp.zeros((3, feature))]
    )
    sent = packed.reshape(8, devices, chunk).transpose(1, 0, 2)
    gathered = lax.all_to_all(sent, "scen", 0, 0, tiled=True).transpose(1, 0, 2)
    mass_all = gathered[4, :, 0]
    member = membership(section_size, rows, devices)
    member_before = membership(section_before, rows, devices)
    total = jnp.sum(member * mass_all, axis=2)
    total_before = jnp.sum(member_before * mass_all, axis=2)
    upper_chunk = lax.dynamic_slice_in_dim(upper, device * chunk, chunk, 1)
    new_chunk = clipped(mixed(member, gathered[0:2]) / total[:, :, None], upper_chunk[:, None])
    source = jnp.where(wide[:, None], (mass_all * product_all)[None, :, None] * new_chunk, gathered[0:2])
    pushed_chunk = mixed(member_before, source) / total_before[:, :, None]
    second_chunk = mixed(member, gathered[2:4]) / total[:, :, None]
    back = jnp.concatenate([new_chunk, second_chunk, pushed_chunk, jnp.zeros((2, devices, chunk))])
    returned = lax.all_to_all(back.transpose(1, 0, 2), "scen", 0, 0, tiled=True)
    returned = returned.transpose(1, 0, 2).reshape(8, 1, feature)
    mean_product = jnp.sum(member[:, device] * (mass_all * product_all), axis=1) / total[:, device]
    new = jnp.where(wide[:, None], returned[0:2], new_local)
    second = jnp.where(wide[:, None], returned[2:4], second_local)
    wide_before = (section_before > rows)[:, None, None]
    weights_before = local_weights(section_before, prob)
    pushed = jnp.where(wide_before, returned[4:6], product * mixed(weights_before, new))
    images = apply_blocks(jnp.concatenate([new, pushed], axis=1), select, pool_tiles)
    new_image = images[:, :rows]
    pulled = 2.0 * (carry * damp[:, None])[:, None] * images[:, rows:]
    pulled_next = jnp.stack([pulled[1], shifted(pulled[0], "per", -1)])
    new_before = jnp.stack([shifted(new[1], "per", 1), new[0]])
    net = 2.0 * (new_image - carry[:, None] * new_before)
    mean_damped = (damp * mean_product)[:, None, None]
    reaction = mean_damped * apply_blocks_transposed(net, select, pool_tiles)
    primal = damp[:, None, None] * new
    averaged = (
        primal + second - reaction + pulled_next
        - 2.0 * square_next[:, None] * mean_product[:, None, None] * new
    )
    primal_new = clipped(averaged, upper[:, None])
    probe = 2.0 * primal_new - primal
    probe_before = jnp.stack([shifted(probe[1], "per", 1), probe[0]])
    change = dual_rate * (target - net)
    dual = start + damp[:, None, None] * change
    dual_new = dual + dual_rate * (
        target - (apply_blocks(probe, select, pool_tiles) - carry[:, None] * probe_before)
    )
    count = jnp.where(restart[0] == 1, 1.0, 2.0)[:, None, None]
    flagged = (restart[1] == 1)[:, None, None]
    primal_mean = (count * (0.5 * new) + primal_new) / (count + 1.0)
    dual_mean = (count * (start + 0.5 * change) + dual_new) / (count + 1.0)
    primal = jnp.where(flagged, primal_mean, primal_new)
    dual = jnp.where(flagged, dual_mean, dual_new)
    return primal.transpose(1, 0, 2), dual.transpose(1, 0, 2)


def solution(mesh):
    return jax.shard_map(
        per_device,
        mesh=mesh,
        in_specs=(
            P("scen", "per", None),
            P("scen", "per", None),
            P("per", None),
            P("per", None),
            P("per", None),
            P("scen"),
            P("per"),
            P("per", None, None),
            P("per", None, None),
            P(),
            P(),
            P(),
            P(None, "per"),
        ),
        out_specs=(P("scen", "per", None), P("scen", "per", None)),
        check_vma=False,
    )
```

```python
import jax
import jax.numpy as jnp
from jax import lax
from jax.experimental import pallas as pl
from jax.experimental.pallas import tpu as pltpu
from jax.sharding import PartitionSpec as P

TILE = 512
NPOOL = 3
NB = 3
SUBTREES = 8
RB = 16
LANES = 128
ROWS = 8
PER = 2
QUARTERS = TILE // LANES
MIB = 1 << 20
F32 = jnp.float32
BF16 = jnp.bfloat16

VM = pl.BlockSpec(memory_space=pltpu.VMEM)
SM = pl.BlockSpec(memory_space=pltpu.SMEM)


def shifted(block, axis, distance):
    devices = range(lax.axis_size(axis))
    route = [(i - distance, i) for i in devices if i - distance in devices]
    return lax.ppermute(block, axis, route)


def call(body, specs, outs, scratch=(), limit=16):
    return pl.pallas_call(
        body,
        out_shape=[jax.ShapeDtypeStruct(shape, dtype) for shape, dtype in outs],
        in_specs=specs,
        out_specs=[VM] * len(outs),
        scratch_shapes=list(scratch),
        compiler_params=pltpu.CompilerParams(vmem_limit_bytes=limit * MIB),
    )


def step_pair(steps_ref, subtree_ref):
    device = lax.axis_index("scen")
    entry = subtree_ref[device // (lax.axis_size("scen") // SUBTREES)]
    return steps_ref[entry, 0], steps_ref[entry, 1]


def damping(restart_ref, period):
    return jnp.where(restart_ref[0, period] == 1, 0.5, 1.0).astype(F32)


def lanes_of(ref, row, block):
    return ref[row : row + 1, block * TILE : (block + 1) * TILE]


def prob_column(prob_ref):
    row = lax.broadcasted_iota(jnp.int32, (ROWS, LANES), 0)
    column = jnp.zeros((ROWS, LANES), F32)
    for s in range(ROWS):
        column = jnp.where(row == s, prob_ref[s], column)
    return column


def widened(column):
    return jnp.concatenate([column] * QUARTERS, axis=1)


def group_sum(values, inside):
    row = lax.broadcasted_iota(jnp.int32, values.shape, 0)
    for step in (1, 2, 4):
        partner = jnp.where(
            (row & step) != 0,
            pltpu.roll(values, step, 0),
            pltpu.roll(values, ROWS - step, 0),
        )
        values = jnp.where(inside > step, values + partner, values)
    return values


def halves(values):
    high = values.astype(BF16)
    return high, (values - high.astype(F32)).astype(BF16)


def product_images(lhs_ref, high_ref, low_ref, image_ref, transposed):
    rows = lhs_ref.shape[0]
    high, low = halves(lhs_ref[...])
    both = jnp.concatenate([high, low], axis=0)
    dims = (((1,), (0,)), ((), ())) if transposed else (((1,), (1,)), ((), ()))

    def dot(a, b):
        return lax.dot_general(a, b, dims, preferred_element_type=F32)

    for j in range(NPOOL):
        main = dot(both, high_ref[j])
        image_ref[j] = main[:rows] + main[rows:] + dot(high, low_ref[j])


def gathered_blocks(image_ref, code_ref, period, block, height):
    total = None
    for k in range(NB):
        code = code_ref[(period * RB + block) * NB + k]
        first = pl.multiple_of((period * RB + code % RB) * height, height)
        part = image_ref[code // RB, pl.ds(first, height), :]
        total = part if total is None else total + part
    return total


def scattered_blocks(image_ref, code_ref, out_ref, height):
    out_ref[...] = jnp.zeros_like(out_ref)
    for period in range(PER):
        for block in range(RB):
            first = (period * RB + block) * height
            for k in range(NB):
                code = code_ref[(period * RB + block) * NB + k]
                part = image_ref[code // RB, first : first + height, :]
                place = pl.multiple_of((period * RB + code % RB) * height, height)
                out_ref[pl.ds(place, height), :] += part


def relayout_kernel(dual_ref, demand_ref, carry_ref, steps_ref, subtree_ref, restart_ref,
                    start_ref, target_ref, carried_ref):
    _, dual_rate = step_pair(steps_ref, subtree_ref)
    for period in range(PER):
        for s in range(ROWS):
            a = dual_ref[s, period : period + 1, :]
            b = demand_ref[s, period : period + 1, :]
            for block in range(RB):
                lanes = slice(block * TILE, (block + 1) * TILE)
                start_ref[period, block, s : s + 1, :] = a[:, lanes]
                target_ref[period, block, s : s + 1, :] = b[:, lanes]
    factor = damping(restart_ref, 0) * dual_rate
    for block in range(RB):
        weight = lanes_of(carry_ref, 0, block)
        a, b = start_ref[0, block], target_ref[0, block]
        carried_ref[block, 0:ROWS, :] = weight * a
        carried_ref[block, ROWS : 2 * ROWS, :] = weight * (a + factor * b)


def pull_kernel(start_ref, target_ref, pool_ref, code_ref, steps_ref, subtree_ref, restart_ref,
                pulled_ref, high_ref, low_ref, lhs_ref, image_ref):
    _, dual_rate = step_pair(steps_ref, subtree_ref)
    for j in range(NPOOL):
        high, low = halves(pool_ref[j])
        high_ref[j] = high
        low_ref[j] = low
    for period in range(PER):
        factor = damping(restart_ref, period) * dual_rate
        for block in range(RB):
            first = (period * RB + block) * 2 * ROWS
            a, b = start_ref[period, block], target_ref[period, block]
            lhs_ref[first : first + ROWS, :] = a
            lhs_ref[first + ROWS : first + 2 * ROWS, :] = a + factor * b
    product_images(lhs_ref, high_ref, low_ref, image_ref, True)
    scattered_blocks(image_ref, code_ref, pulled_ref, 2 * ROWS)


def local_kernel(pulled_ref, start_ref, target_ref, arriving_ref, cost_ref, upper_ref, carry_ref,
                 prob_ref, section_ref, steps_ref, subtree_ref, restart_ref,
                 new_ref, second_ref, message_ref):
    rate, dual_rate = step_pair(steps_ref, subtree_ref)
    product = rate * dual_rate
    narrow = prob_column(prob_ref)
    mass = jnp.sum(narrow, axis=0, keepdims=True)
    weight = widened(narrow)
    total_mass = widened(mass)
    factor = damping(restart_ref, 1) * dual_rate
    for period in range(PER):
        section = section_ref[period]
        inverse = 1.0 / group_sum(weight, section)
        wide = section > ROWS
        for block in range(RB):
            first = (period * RB + block) * 2 * ROWS
            if period == 0:
                carry = lanes_of(carry_ref, 1, block)
                a = start_ref[1, block]
                follow_first = carry * a
                follow_second = carry * (a + factor * target_ref[1, block])
            else:
                follow_first = arriving_ref[block, 0:ROWS, :]
                follow_second = arriving_ref[block, ROWS : 2 * ROWS, :]
            cost = lanes_of(cost_ref, period, block)
            raw = rate * (pulled_ref[first : first + ROWS, :] - follow_first - cost)
            other = rate * (pulled_ref[first + ROWS : first + 2 * ROWS, :] - follow_second - cost)
            averaged = group_sum(weight * raw, section) * inverse
            second = group_sum(weight * other, section) * inverse
            new = jnp.minimum(jnp.maximum(averaged, 0.0), lanes_of(upper_ref, period, block))
            new_ref[period, block] = new
            second_ref[period, block] = second
            pushed = product * jnp.sum(weight * new, axis=0, keepdims=True)
            sums = jnp.where(wide, total_mass * averaged[0:1], pushed)
            second_sums = total_mass * second[0:1]
            for quarter in range(QUARTERS):
                lanes = slice(quarter * LANES, (quarter + 1) * LANES)
                chunk = block * QUARTERS + quarter
                message_ref[chunk, period : period + 1, :] = sums[:, lanes]
                message_ref[chunk, 2 + period : 3 + period, :] = second_sums[:, lanes]
    for chunk in range(RB * QUARTERS):
        message_ref[chunk, 4:5, :] = mass
        message_ref[chunk, 5:6, :] = product * mass
        message_ref[chunk, 6:8, :] = jnp.zeros((2, LANES), F32)


def reduce_kernel(got_ref, upper_ref, section_ref, before_ref, back_ref):
    devices = got_ref.shape[0]
    row = lax.broadcasted_iota(jnp.int32, (devices, devices), 0)
    column = lax.broadcasted_iota(jnp.int32, (devices, devices), 1)

    def member(section):
        span = jnp.maximum(section // ROWS, 1)
        return ((row & -span) == (column & -span)).astype(F32)

    def dot(a, b):
        return jnp.dot(a, b, precision=lax.Precision.HIGHEST, preferred_element_type=F32)

    place = pl.multiple_of(lax.axis_index("scen") * LANES, LANES)
    mass = got_ref[:, 4, :]
    moment = got_ref[:, 5, :]
    sections = (section_ref[0], section_ref[1])
    befores = (before_ref[0], section_ref[0])
    for period in range(PER):
        same = member(sections[period])
        inverse = 1.0 / dot(same, mass)
        sums = got_ref[:, period, :]
        upper = upper_ref[period : period + 1, pl.ds(place, LANES)]
        new = jnp.minimum(jnp.maximum(dot(same, sums) * inverse, 0.0), upper)
        back_ref[:, period, :] = new
        back_ref[:, 2 + period, :] = dot(same, got_ref[:, 2 + period, :]) * inverse
        back_ref[:, 6 + period, :] = dot(same, moment) * inverse
        source = jnp.where(sections[period] > ROWS, moment * new, sums)
        same = member(befores[period])
        back_ref[:, 4 + period, :] = dot(same, source) / dot(same, mass)


def row_of(returned_ref, index, block):
    parts = [
        returned_ref[block * QUARTERS + quarter, index : index + 1, :] for quarter in range(QUARTERS)
    ]
    return jnp.concatenate(parts, axis=1)


def select_kernel(returned_ref, local_ref, local_second_ref, prob_ref, section_ref, before_ref,
                  steps_ref, subtree_ref, early_ref, late_ref, second_ref, pushed_ref):
    rate, dual_rate = step_pair(steps_ref, subtree_ref)
    product = rate * dual_rate
    weight = widened(prob_column(prob_ref))
    befores = (before_ref[0], section_ref[0])
    for period in range(PER):
        out_ref = (early_ref, late_ref)[period]
        wide = section_ref[period] > ROWS
        wide_before = befores[period] > ROWS
        scale = product / group_sum(weight, befores[period])
        for block in range(RB):
            shape = (ROWS, TILE)
            row = jnp.broadcast_to(row_of(returned_ref, period, block), shape)
            new = jnp.where(wide, row, local_ref[period, block])
            out_ref[block] = new
            row = jnp.broadcast_to(row_of(returned_ref, 2 + period, block), shape)
            second_ref[period, block] = jnp.where(wide, row, local_second_ref[period, block])
            row = jnp.broadcast_to(row_of(returned_ref, 4 + period, block), shape)
            averaged = scale * group_sum(weight * new, befores[period])
            pushed_ref[period, block] = jnp.where(wide_before, row, averaged)


def push_kernel(early_ref, late_ref, pushed_ref, high_ref, low_ref, code_ref, carry_ref, restart_ref,
                image_out_ref, first_ref, next_ref, lhs_ref, image_ref):
    for period in range(PER):
        new_ref = (early_ref, late_ref)[period]
        for block in range(RB):
            first = (period * RB + block) * 2 * ROWS
            lhs_ref[first : first + ROWS, :] = new_ref[block]
            lhs_ref[first + ROWS : first + 2 * ROWS, :] = pushed_ref[period, block]
    product_images(lhs_ref, high_ref, low_ref, image_ref, False)
    for period in range(PER):
        out_ref = (first_ref, next_ref)[period]
        factor = 2.0 * damping(restart_ref, period)
        for block in range(RB):
            both = gathered_blocks(image_ref, code_ref, period, block, 2 * ROWS)
            image_out_ref[period, block] = both[:ROWS]
            out_ref[block] = factor * lanes_of(carry_ref, period, block) * both[ROWS:]


def second_kernel(early_ref, late_ref, before_ref, images_ref, second_ref, near_ref, far_ref,
                  returned_ref, square_ref, upper_ref, carry_ref, high_ref, low_ref, code_ref,
                  restart_ref, net_ref, primal_ref, early_probe_ref, late_probe_ref,
                  lhs_ref, image_ref, pulled_ref):
    for period in range(PER):
        previous_ref = (before_ref, early_ref)[period]
        damp = damping(restart_ref, period)
        for block in range(RB):
            carry = lanes_of(carry_ref, period, block)
            net = 2.0 * (images_ref[period, block] - carry * previous_ref[block])
            net_ref[period, block] = net
            first = (period * RB + block) * ROWS
            lhs_ref[first : first + ROWS, :] = damp * row_of(returned_ref, 6 + period, block) * net
    product_images(lhs_ref, high_ref, low_ref, image_ref, True)
    scattered_blocks(image_ref, code_ref, pulled_ref, ROWS)
    damp_late = damping(restart_ref, 1)
    for period in range(PER):
        new_ref = (early_ref, late_ref)[period]
        next_ref = (near_ref, far_ref)[period]
        probe_ref = (early_probe_ref, late_probe_ref)[period]
        damp = damping(restart_ref, period)
        for block in range(RB):
            if period == 0:
                carry = lanes_of(carry_ref, 1, block)
                square = damp_late * carry * carry
            else:
                square = lanes_of(square_ref, 0, block)
            first = (period * RB + block) * ROWS
            new = new_ref[block]
            primal = damp * new
            averaged = (
                primal + second_ref[period, block] - pulled_ref[first : first + ROWS, :]
                + next_ref[block]
                - 2.0 * square * row_of(returned_ref, 6 + period, block) * new
            )
            primal_new = jnp.minimum(jnp.maximum(averaged, 0.0), lanes_of(upper_ref, period, block))
            primal_ref[period, block] = primal_new
            probe_ref[block] = 2.0 * primal_new - primal


def probe_kernel(early_ref, late_ref, high_ref, low_ref, code_ref, out_ref, lhs_ref, image_ref):
    for period in range(PER):
        probe_ref = (early_ref, late_ref)[period]
        for block in range(RB):
            first = (period * RB + block) * ROWS
            lhs_ref[first : first + ROWS, :] = probe_ref[block]
    product_images(lhs_ref, high_ref, low_ref, image_ref, False)
    for period in range(PER):
        for block in range(RB):
            out_ref[period, block] = gathered_blocks(image_ref, code_ref, period, block, ROWS)


def final_kernel(image_ref, early_probe_ref, before_ref, start_ref, target_ref, net_ref,
                 early_ref, late_ref, new_ref, carry_ref, steps_ref, subtree_ref, restart_ref,
                 primal_ref, dual_ref):
    _, dual_rate = step_pair(steps_ref, subtree_ref)
    for period in range(PER):
        previous_ref = (before_ref, early_probe_ref)[period]
        first_ref = (early_ref, late_ref)[period]
        damp = damping(restart_ref, period)
        count = jnp.where(restart_ref[0, period] == 1, 1.0, 2.0).astype(F32)
        flagged = restart_ref[1, period] == 1
        share = 1.0 / (count + jnp.ones((ROWS, TILE), F32))
        for block in range(RB):
            start, target = start_ref[period, block], target_ref[period, block]
            change = dual_rate * (target - net_ref[period, block])
            carry = lanes_of(carry_ref, period, block)
            image = image_ref[period, block] - carry * previous_ref[block]
            dual_new = start + damp * change + dual_rate * (target - image)
            dual_mean = (count * (start + 0.5 * change) + dual_new) * share
            primal_new = new_ref[period, block]
            primal_mean = (count * (0.5 * first_ref[block]) + primal_new) * share
            primal = jnp.where(flagged, primal_mean, primal_new)
            dual = jnp.where(flagged, dual_mean, dual_new)
            lanes = slice(block * TILE, (block + 1) * TILE)
            for s in range(ROWS):
                primal_ref[s, period : period + 1, lanes] = primal[s : s + 1]
                dual_ref[s, period : period + 1, lanes] = dual[s : s + 1]


def per_device(
    dual_start,
    demand,
    cost,
    upper,
    carry,
    prob,
    section_size,
    block_cols,
    block_pool,
    pool_tiles,
    step_table,
    subtree_step,
    restart,
):
    rows, periods, feature = dual_start.shape
    devices = lax.axis_size("scen")
    field = (PER, RB, ROWS, TILE)
    slab = (RB, ROWS, TILE)
    tiles = (NPOOL, TILE, TILE)
    exchange = (devices, 8, LANES)
    code = (block_pool * RB + block_cols).reshape(PER * RB * NB)
    steps = (step_table, subtree_step)

    def scratch(height):
        count = PER * RB * height
        return [pltpu.VMEM((count, TILE), F32), pltpu.VMEM((NPOOL, count, TILE), F32)]

    with jax.named_scope("relayout"):
        start, target, carried = call(
            relayout_kernel, [VM] * 3 + [SM] * 3,
            [(field, F32), (field, F32), ((RB, 2 * ROWS, TILE), F32)],
        )(dual_start, demand, carry, *steps, restart)
    arriving = shifted(carried, "per", -1)
    with jax.named_scope("first_pull"):
        pulled, high, low = call(
            pull_kernel, [VM] * 3 + [SM] * 4,
            [((PER * RB * 2 * ROWS, TILE), F32), (tiles, BF16), (tiles, BF16)],
            scratch(2 * ROWS), 32,
        )(start, target, pool_tiles, code, *steps, restart)
    with jax.named_scope("local_average"):
        local, local_second, message = call(
            local_kernel, [VM] * 7 + [SM] * 5, [(field, F32), (field, F32), (exchange, F32)],
        )(pulled, start, target, arriving, cost, upper, carry, prob, section_size, *steps, restart)
    late_section, late_square, message = lax.optimization_barrier(
        (section_size[1:], carry[0:1] * carry[0:1] * jnp.where(restart[0, 0] == 1, 0.5, 1.0), message)
    )
    got = lax.all_to_all(message, "scen", 0, 0, tiled=True)
    before = shifted(late_section, "per", 1)
    square = shifted(late_square, "per", -1)
    with jax.named_scope("section_average"):
        (back,) = call(reduce_kernel, [VM] * 2 + [SM] * 2, [(exchange, F32)])(
            got, upper, section_size, before
        )
    returned = lax.all_to_all(back, "scen", 0, 0, tiled=True)
    with jax.named_scope("selected"):
        early, late, second, pushed = call(
            select_kernel, [VM] * 3 + [SM] * 5,
            [(slab, F32), (slab, F32), (field, F32), (field, F32)],
        )(returned, local, local_second, prob, section_size, before, *steps)
    new_before = shifted(late, "per", 1)
    with jax.named_scope("push"):
        images, first, near = call(
            push_kernel, [VM] * 5 + [SM] + [VM] + [SM],
            [(field, F32), (slab, F32), (slab, F32)], scratch(2 * ROWS), 32,
        )(early, late, pushed, high, low, code, carry, restart)
    far = shifted(first, "per", -1)
    with jax.named_scope("second_pull"):
        net, primal_new, early_probe, late_probe = call(
            second_kernel, [VM] * 13 + [SM] * 2,
            [(field, F32), (field, F32), (slab, F32), (slab, F32)],
            scratch(ROWS) + [pltpu.VMEM((PER * RB * ROWS, TILE), F32)], 32,
        )(early, late, new_before, images, second, near, far, returned, square, upper, carry,
          high, low, code, restart)
    probe_before = shifted(late_probe, "per", 1)
    with jax.named_scope("second_push"):
        (image,) = call(
            probe_kernel, [VM] * 4 + [SM], [(field, F32)], scratch(ROWS), 32,
        )(early_probe, late_probe, high, low, code)
    with jax.named_scope("result"):
        primal, dual = call(
            final_kernel, [VM] * 10 + [SM] * 3, [(dual_start.shape, F32), (dual_start.shape, F32)],
        )(image, early_probe, probe_before, start, target, net, early, late, primal_new, carry,
          *steps, restart)
    return primal, dual


def solution(mesh):
    return jax.shard_map(
        per_device,
        mesh=mesh,
        in_specs=(
            P("scen", "per", None),
            P("scen", "per", None),
            P("per", None),
            P("per", None),
            P("per", None),
            P("scen"),
            P("per"),
            P("per", None, None),
            P("per", None, None),
            P(),
            P(),
            P(),
            P(None, "per"),
        ),
        out_specs=(P("scen", "per", None), P("scen", "per", None)),
        check_vma=False,
    )
```

```python
import jax
import jax.numpy as jnp
from jax import lax
from jax.experimental import pallas as pl
from jax.experimental.pallas import tpu as pltpu
from jax.sharding import PartitionSpec as P

TILE = 512
NPOOL = 3
NB = 3
SUBTREES = 8
RB = 16
LANES = 128
ROWS = 8
PER = 2
QUARTERS = TILE // LANES
MIB = 1 << 20
F32 = jnp.float32
BF16 = jnp.bfloat16

VM = pl.BlockSpec(memory_space=pltpu.VMEM)
SM = pl.BlockSpec(memory_space=pltpu.SMEM)
FAR = pl.BlockSpec(memory_space=pltpu.HBM)
PROB, RATE, DUAL_RATE, DAMP, FLAG, SECTION, PRODUCTS, TABLE = 0, 1, 2, 3, 5, 7, 9, 17


def shifted(block, axis, distance):
    devices = range(lax.axis_size(axis))
    route = [(i - distance, i) for i in devices if i - distance in devices]
    return lax.ppermute(block, axis, route)


def call(body, specs, outs, scratch=(), limit=4, aliases={}, places=None):
    return pl.pallas_call(
        body,
        input_output_aliases=aliases,
        out_shape=[jax.ShapeDtypeStruct(shape, dtype) for shape, dtype in outs],
        in_specs=specs,
        out_specs=places or [VM] * len(outs),
        scratch_shapes=list(scratch),
        compiler_params=pltpu.CompilerParams(vmem_limit_bytes=limit * MIB),
    )


def lanes_of(ref, row, block):
    return ref[row : row + 1, block * TILE : (block + 1) * TILE]


def widened(column):
    return jnp.concatenate([column] * QUARTERS, axis=1)


def entry_of(table_ref, index):
    return widened(table_ref[index])


def group_sum(values, inside):
    row = lax.broadcasted_iota(jnp.int32, values.shape, 0)
    for step in (1, 2, 4):
        partner = jnp.where(
            (row & step) != 0,
            pltpu.roll(values, step, 0),
            pltpu.roll(values, ROWS - step, 0),
        )
        values = jnp.where(inside > step, values + partner, values)
    return values


def halves(values):
    high = values.astype(BF16)
    return high, (values - high.astype(F32)).astype(BF16)


def product_images(lhs_ref, high_ref, low_ref, image_ref, transposed, ready=None):
    rows = lhs_ref.shape[0]
    high, low = halves(lhs_ref[...])
    both = jnp.concatenate([high, low], axis=0)
    dims = (((1,), (0,)), ((), ())) if transposed else (((1,), (1,)), ((), ()))

    def dot(a, b):
        return lax.dot_general(a, b, dims, preferred_element_type=F32)

    for j in range(NPOOL):
        if ready is not None:
            ready(j)
        main = dot(both, high_ref[j])
        image_ref[j] = main[:rows] + main[rows:] + dot(high, low_ref[j])


def gathered_blocks(image_ref, code_ref, period, block, height):
    total = None
    for k in range(NB):
        code = code_ref[(period * RB + block) * NB + k]
        first = pl.multiple_of((period * RB + code % RB) * height, height)
        part = image_ref[code // RB, pl.ds(first, height), :]
        total = part if total is None else total + part
    return total


def scattered_blocks(image_ref, code_ref, out_ref, height):
    out_ref[...] = jnp.zeros_like(out_ref)
    for period in range(PER):
        for block in range(RB):
            first = (period * RB + block) * height
            for k in range(NB):
                code = code_ref[(period * RB + block) * NB + k]
                part = image_ref[code // RB, first : first + height, :]
                place = pl.multiple_of((period * RB + code % RB) * height, height)
                out_ref[pl.ds(place, height), :] += part


def fetch(pairs, sems):
    copies = [
        pltpu.make_async_copy(source, place, sems.at[i]) for i, (source, place) in enumerate(pairs)
    ]
    for copy in copies:
        copy.start()
    return copies


def carried_kernel(dual_hbm, demand_hbm, carry_hbm, prob_hbm, section_hbm, steps_hbm, subtree_hbm,
                   restart_hbm, carried_ref, square_ref, table_ref,
                   dual_ref, demand_ref, carry_ref, prob_ref, section_ref, steps_ref, subtree_ref,
                   restart_ref, first_ref, other_ref, sems):
    copies = fetch(
        [(prob_hbm, prob_ref), (section_hbm, section_ref), (steps_hbm, steps_ref),
         (subtree_hbm, subtree_ref), (restart_hbm, restart_ref), (carry_hbm, carry_ref),
         (dual_hbm, dual_ref), (demand_hbm, demand_ref)], sems)
    for copy in copies[:6]:
        copy.wait()
    device = lax.axis_index("scen")
    share = lax.axis_size("scen") // SUBTREES
    shape = (ROWS, LANES)
    row = lax.broadcasted_iota(jnp.int32, shape, 0)
    column = jnp.zeros(shape, F32)
    for s in range(ROWS):
        column = jnp.where(row == s, prob_ref[s], column)
    entry = subtree_ref[device // share]
    rate, dual_rate = steps_ref[0, entry], steps_ref[1, entry]
    table_ref[PROB] = column
    table_ref[RATE] = jnp.full(shape, rate)
    table_ref[DUAL_RATE] = jnp.full(shape, dual_rate)
    damps = []
    for period in range(PER):
        damps.append(jnp.where(restart_ref[0, period] == 1, 0.5, 1.0).astype(F32))
        table_ref[DAMP + period] = jnp.full(shape, damps[period])
        table_ref[FLAG + period] = jnp.full(shape, restart_ref[1, period].astype(F32))
        table_ref[SECTION + period] = jnp.full(shape, section_ref[period].astype(F32))
    assert share == ROWS
    for subtree in range(SUBTREES):
        other = subtree_ref[subtree]
        value = steps_ref[0, other] * steps_ref[1, other]
        table_ref[PRODUCTS + subtree] = jnp.full(shape, value)
    carry = carry_ref[0:1, :]
    square_ref[...] = damps[0] * carry * carry
    for copy in copies[6:]:
        copy.wait()
    for s in range(ROWS):
        a, b = dual_ref[s, 0:1, :], demand_ref[s, 0:1, :]
        for block in range(RB):
            lanes = slice(block * TILE, (block + 1) * TILE)
            first_ref[block, s : s + 1, :] = a[:, lanes]
            other_ref[block, s : s + 1, :] = b[:, lanes]
    factor = damps[0] * dual_rate
    for block in range(RB):
        weight = lanes_of(carry_ref, 0, block)
        a = first_ref[block]
        carried_ref[block, 0:ROWS, :] = weight * a
        carried_ref[block, ROWS : 2 * ROWS, :] = weight * (a + factor * other_ref[block])


def pull_kernel(dual_hbm, demand_hbm, pool_hbm, carry_hbm, cost_hbm, table_ref, code_ref,
                raw_ref, high_ref, low_ref,
                dual_ref, demand_ref, pool_ref, carry_ref, cost_ref, lhs_ref, image_ref, sems):
    copies = fetch(
        [(dual_hbm, dual_ref), (demand_hbm, demand_ref)]
        + [(pool_hbm.at[j], pool_ref.at[j]) for j in range(NPOOL)]
        + [(carry_hbm, carry_ref), (cost_hbm, cost_ref)], sems)
    copies[0].wait()
    copies[1].wait()
    for period in range(PER):
        factor = table_ref[DAMP + period, 0:1, 0:1] * table_ref[DUAL_RATE, 0:1, 0:1]
        for s in range(ROWS):
            a = dual_ref[s, period : period + 1, :]
            moved = a + factor * demand_ref[s, period : period + 1, :]
            for block in range(RB):
                lanes = slice(block * TILE, (block + 1) * TILE)
                first = (period * RB + block) * 2 * ROWS + s
                lhs_ref[first : first + 1, :] = a[:, lanes]
                lhs_ref[first + ROWS : first + ROWS + 1, :] = moved[:, lanes]

    def ready(j):
        copies[2 + j].wait()
        high, low = halves(pool_ref[j])
        high_ref[j] = high
        low_ref[j] = low

    product_images(lhs_ref, high_ref, low_ref, image_ref, True, ready)
    scattered_blocks(image_ref, code_ref, raw_ref, 2 * ROWS)
    copies[5].wait()
    copies[6].wait()
    rate = jnp.concatenate([entry_of(table_ref, RATE)] * 2, axis=0)
    for period in range(PER):
        for block in range(RB):
            first = (period * RB + block) * 2 * ROWS
            here = slice(first, first + 2 * ROWS)
            value = raw_ref[here, :] - lanes_of(cost_ref, period, block)
            if period == 0:
                later = (RB + block) * 2 * ROWS
                value -= lanes_of(carry_ref, 1, block) * lhs_ref[later : later + 2 * ROWS, :]
            raw_ref[here, :] = rate * value


def local_kernel(raw_ref, arriving_ref, upper_ref, table_ref,
                 new_hbm, second_hbm, message_ref, chunk_ref, new_ref, second_ref, sems):
    place = pl.multiple_of(lax.axis_index("scen") * LANES, LANES)
    copies = []
    rate = entry_of(table_ref, RATE)
    product = rate * entry_of(table_ref, DUAL_RATE)
    weight = entry_of(table_ref, PROB)
    mass = jnp.sum(weight, axis=0, keepdims=True)
    for period in range(PER):
        section = entry_of(table_ref, SECTION + period)
        inverse = 1.0 / group_sum(weight, section)
        wide = section[0:1] > ROWS
        for block in range(RB):
            first = (period * RB + block) * 2 * ROWS
            raw = raw_ref[first : first + ROWS, :]
            other = raw_ref[first + ROWS : first + 2 * ROWS, :]
            if period == 1:
                raw -= rate * arriving_ref[block, 0:ROWS, :]
                other -= rate * arriving_ref[block, ROWS : 2 * ROWS, :]
            averaged = group_sum(weight * raw, section) * inverse
            second = group_sum(weight * other, section) * inverse
            new = jnp.minimum(jnp.maximum(averaged, 0.0), lanes_of(upper_ref, period, block))
            new_ref[period, block] = new
            second_ref[period, block] = second
            pushed = jnp.sum(product * weight * new, axis=0, keepdims=True)
            sums = jnp.where(wide, mass * averaged[0:1], pushed)
            second_sums = mass * second[0:1]
            for quarter in range(QUARTERS):
                lanes = slice(quarter * LANES, (quarter + 1) * LANES)
                chunk = block * QUARTERS + quarter
                message_ref[chunk, period : period + 1, :] = sums[:, lanes]
                message_ref[chunk, 2 + period : 3 + period, :] = second_sums[:, lanes]
        chunk_ref[period] = jnp.broadcast_to(
            upper_ref[period : period + 1, pl.ds(place, LANES)], (ROWS, LANES)
        )
        for i, (source, out) in enumerate(((new_ref, new_hbm), (second_ref, second_hbm))):
            copy = pltpu.make_async_copy(
                source.at[period], out.at[period], sems.at[2 * period + i]
            )
            copy.start()
            copies.append(copy)
    for chunk in range(RB * QUARTERS):
        message_ref[chunk, 4:5, :] = mass[:, :LANES]
    for copy in copies:
        copy.wait()


def reduce_kernel(got_ref, upper_ref, table_ref, before_ref, back_ref, mean_ref, moment_ref):
    devices = got_ref.shape[0]
    row = lax.broadcasted_iota(jnp.int32, (devices, devices), 0)
    column = lax.broadcasted_iota(jnp.int32, (devices, devices), 1)

    def member(section):
        span = jnp.maximum(section[0:1, 0:devices].astype(jnp.int32) // ROWS, 1)
        return ((row & -span) == (column & -span)).astype(F32)

    def dot(a, b):
        return jnp.dot(a, b, precision=lax.Precision.HIGHEST, preferred_element_type=F32)

    device = lax.axis_index("scen")
    mass = got_ref[:, 4, :]
    moment = mass * table_ref[PRODUCTS:TABLE].reshape(devices, LANES)
    befores = (before_ref[...], table_ref[SECTION])
    for period in range(PER):
        section = table_ref[SECTION + period]
        same = member(section)
        inverse = 1.0 / dot(same, mass)
        sums = got_ref[:, period, :]
        upper = upper_ref[period, 0:1, :]
        new = jnp.minimum(jnp.maximum(dot(same, sums) * inverse, 0.0), upper)
        back_ref[:, period, :] = new
        back_ref[:, 2 + period, :] = dot(same, got_ref[:, 2 + period, :]) * inverse
        moment_ref[...] = dot(same, moment) * inverse
        mean_ref[period] = jnp.broadcast_to(moment_ref[pl.ds(device, 1), :], (ROWS, LANES))
        source = jnp.where(section[0:1] > ROWS, moment * new, sums)
        same = member(befores[period])
        back_ref[:, 4 + period, :] = dot(same, source) / dot(same, mass)


def row_of(returned_ref, index, block):
    parts = [
        returned_ref[block * QUARTERS + quarter, index : index + 1, :] for quarter in range(QUARTERS)
    ]
    return jnp.concatenate(parts, axis=1)


def select_kernel(returned_ref, local_hbm, local_second_hbm, table_ref, before_ref,
                  early_ref, late_ref, second_ref, pushed_ref, local_ref, local_second_ref, sems):
    copies = fetch([(local_hbm, local_ref), (local_second_hbm, local_second_ref)], sems)
    for copy in copies:
        copy.wait()
    product = entry_of(table_ref, RATE) * entry_of(table_ref, DUAL_RATE)
    weight = entry_of(table_ref, PROB)
    befores = (widened(before_ref[...]), entry_of(table_ref, SECTION))
    for period in range(PER):
        out_ref = (early_ref, late_ref)[period]
        wide = entry_of(table_ref, SECTION + period) > ROWS
        wide_before = befores[period] > ROWS
        scale = product / group_sum(weight, befores[period])
        for block in range(RB):
            shape = (ROWS, TILE)
            row = jnp.broadcast_to(row_of(returned_ref, period, block), shape)
            new = jnp.where(wide, row, local_ref[period, block])
            out_ref[block] = new
            row = jnp.broadcast_to(row_of(returned_ref, 2 + period, block), shape)
            second_ref[period, block] = jnp.where(wide, row, local_second_ref[period, block])
            row = jnp.broadcast_to(row_of(returned_ref, 4 + period, block), shape)
            averaged = scale * group_sum(weight * new, befores[period])
            pushed_ref[period, block] = jnp.where(wide_before, row, averaged)


def push_kernel(early_ref, late_ref, pushed_ref, high_ref, low_ref, carry_ref, table_ref, code_ref,
                image_out_ref, first_ref, next_ref, lhs_ref, image_ref):
    for period in range(PER):
        new_ref = (early_ref, late_ref)[period]
        for block in range(RB):
            first = (period * RB + block) * 2 * ROWS
            lhs_ref[first : first + ROWS, :] = new_ref[block]
            lhs_ref[first + ROWS : first + 2 * ROWS, :] = pushed_ref[period, block]
    product_images(lhs_ref, high_ref, low_ref, image_ref, False)
    for period in range(PER):
        out_ref = (first_ref, next_ref)[period]
        factor = 2.0 * entry_of(table_ref, DAMP + period)
        for block in range(RB):
            both = gathered_blocks(image_ref, code_ref, period, block, 2 * ROWS)
            image_out_ref[period, block] = both[:ROWS]
            out_ref[block] = factor * lanes_of(carry_ref, period, block) * both[ROWS:]


def second_kernel(early_ref, late_ref, before_ref, images_ref, second_ref, near_ref, far_ref,
                  mean_ref, square_ref, upper_ref, carry_ref, high_ref, low_ref, table_ref, code_ref,
                  net_ref, primal_ref, early_probe_ref, late_probe_ref,
                  lhs_ref, image_ref, pulled_ref):
    for period in range(PER):
        previous_ref = (before_ref, early_ref)[period]
        factor = entry_of(table_ref, DAMP + period) * widened(mean_ref[period])
        for block in range(RB):
            carry = lanes_of(carry_ref, period, block)
            net = 2.0 * (images_ref[period, block] - carry * previous_ref[block])
            net_ref[period, block] = net
            first = (period * RB + block) * ROWS
            lhs_ref[first : first + ROWS, :] = factor * net
    product_images(lhs_ref, high_ref, low_ref, image_ref, True)
    scattered_blocks(image_ref, code_ref, pulled_ref, ROWS)
    for period in range(PER):
        new_ref = (early_ref, late_ref)[period]
        next_ref = (near_ref, far_ref)[period]
        probe_ref = (early_probe_ref, late_probe_ref)[period]
        damp = entry_of(table_ref, DAMP + period)
        mean = 2.0 * widened(mean_ref[period])
        if period == 0:
            mean *= entry_of(table_ref, DAMP + 1)
        for block in range(RB):
            if period == 0:
                carry = lanes_of(carry_ref, 1, block)
                square = carry * carry
            else:
                square = lanes_of(square_ref, 0, block)
            first = (period * RB + block) * ROWS
            new = new_ref[block]
            primal = damp * new
            averaged = (
                primal + second_ref[period, block] - pulled_ref[first : first + ROWS, :]
                + next_ref[block] - square * mean * new
            )
            primal_new = jnp.minimum(jnp.maximum(averaged, 0.0), lanes_of(upper_ref, period, block))
            primal_ref[period, block] = primal_new
            probe_ref[block] = 2.0 * primal_new - primal


def result_kernel(early_probe_ref, late_probe_ref, high_ref, low_ref, dual_ref, demand_ref, net_ref,
                  early_ref, late_ref, new_ref, carry_ref, table_ref, code_ref,
                  primal_ref, out_ref, lhs_ref, image_ref, start_ref, target_ref):
    for period in range(PER):
        probe_ref = (early_probe_ref, late_probe_ref)[period]
        for block in range(RB):
            first = (period * RB + block) * ROWS
            lhs_ref[first : first + ROWS, :] = probe_ref[block]
        for s in range(ROWS):
            a = dual_ref[s, period : period + 1, :]
            b = demand_ref[s, period : period + 1, :]
            for block in range(RB):
                lanes = slice(block * TILE, (block + 1) * TILE)
                start_ref[period, block, s : s + 1, :] = a[:, lanes]
                target_ref[period, block, s : s + 1, :] = b[:, lanes]
    product_images(lhs_ref, high_ref, low_ref, image_ref, False)
    dual_rate = entry_of(table_ref, DUAL_RATE)
    for period in range(PER):
        first_ref = (early_ref, late_ref)[period]
        damp = entry_of(table_ref, DAMP + period)
        count = 2.0 * damp
        flagged = entry_of(table_ref, FLAG + period) == 1.0
        share = 1.0 / (count + 1.0)
        for block in range(RB):
            start, target = start_ref[period, block], target_ref[period, block]
            change = dual_rate * (target - net_ref[period, block])
            image = gathered_blocks(image_ref, code_ref, period, block, ROWS)
            if period == 1:
                image -= lanes_of(carry_ref, 1, block) * early_probe_ref[block]
            dual_new = start + damp * change + dual_rate * (target - image)
            dual_mean = (count * (start + 0.5 * change) + dual_new) * share
            primal_new = new_ref[period, block]
            primal_mean = (count * (0.5 * first_ref[block]) + primal_new) * share
            primal = jnp.where(flagged, primal_mean, primal_new)
            dual = jnp.where(flagged, dual_mean, dual_new)
            lanes = slice(block * TILE, (block + 1) * TILE)
            for s in range(ROWS):
                primal_ref[s, period : period + 1, lanes] = primal[s : s + 1]
                out_ref[s, period : period + 1, lanes] = dual[s : s + 1]


def correct_kernel(partial_ref, before_ref, carry_ref, table_ref, out_ref):
    share = 1.0 / (2.0 * entry_of(table_ref, DAMP) + 1.0)
    factor = entry_of(table_ref, DUAL_RATE) * jnp.where(
        entry_of(table_ref, FLAG) == 1.0, share, 1.0
    )
    for block in range(RB):
        added = factor * lanes_of(carry_ref, 0, block) * before_ref[block]
        lanes = slice(block * TILE, (block + 1) * TILE)
        for s in range(ROWS):
            out_ref[s, 0:1, lanes] = partial_ref[s, 0:1, lanes] + added[s : s + 1]
            out_ref[s, 1:2, lanes] = partial_ref[s, 1:2, lanes]


def per_device(
    dual_start,
    demand,
    cost,
    upper,
    carry,
    prob,
    section_size,
    block_cols,
    block_pool,
    pool_tiles,
    step_table,
    subtree_step,
    restart,
):
    rows, periods, feature = dual_start.shape
    devices = lax.axis_size("scen")
    field = (PER, RB, ROWS, TILE)
    slab = (RB, ROWS, TILE)
    tiles = (NPOOL, TILE, TILE)
    packed = (PER, feature)
    code = (block_pool * RB + block_cols).reshape(PER * RB * NB)

    def scratch(height):
        count = PER * RB * height
        return [pltpu.VMEM((count, TILE), F32), pltpu.VMEM((NPOOL, count, TILE), F32)]

    with jax.named_scope("carried"):
        carried, square, table = call(
            carried_kernel, [FAR] * 8,
            [((RB, 2 * ROWS, TILE), F32), ((1, feature), F32), ((TABLE, ROWS, LANES), F32)],
            [pltpu.VMEM(dual_start.shape, F32), pltpu.VMEM(dual_start.shape, F32),
             pltpu.VMEM(packed, F32), pltpu.SMEM((ROWS,), F32), pltpu.SMEM((PER,), jnp.int32),
             pltpu.SMEM(step_table.shape[::-1], F32), pltpu.SMEM((SUBTREES,), jnp.int32),
             pltpu.SMEM(restart.shape, jnp.int32), pltpu.VMEM(slab, F32), pltpu.VMEM(slab, F32),
             pltpu.SemaphoreType.DMA((8,))], 60,
        )(dual_start, demand, carry, prob, section_size, step_table.T, subtree_step, restart)
    arriving = shifted(carried, "per", -1)
    with jax.named_scope("first_pull"):
        raw, high, low = call(
            pull_kernel, [FAR] * 5 + [VM, SM],
            [((PER * RB * 2 * ROWS, TILE), F32), (tiles, BF16), (tiles, BF16)],
            [pltpu.VMEM(dual_start.shape, F32), pltpu.VMEM(dual_start.shape, F32),
             pltpu.VMEM(tiles, F32), pltpu.VMEM(packed, F32), pltpu.VMEM(packed, F32)]
            + scratch(2 * ROWS) + [pltpu.SemaphoreType.DMA((7,))], 60,
        )(dual_start, demand, pool_tiles, carry, cost, table, code)
    with jax.named_scope("local_average"):
        local, local_second, message, upper_chunk = call(
            local_kernel, [VM] * 4,
            [(field, F32), (field, F32), ((devices, 5, LANES), F32), ((PER, ROWS, LANES), F32)],
            [pltpu.VMEM(field, F32), pltpu.VMEM(field, F32), pltpu.SemaphoreType.DMA((4,))],
            places=[FAR, FAR, VM, VM],
        )(raw, arriving, upper, table)
    late_section, late_square, message = lax.optimization_barrier(
        (table[SECTION + 1], square, message)
    )
    got = lax.all_to_all(message, "scen", 0, 0, tiled=True)
    before = shifted(late_section, "per", 1)
    square_next = shifted(late_square, "per", -1)
    before, square_next, got = lax.optimization_barrier((before, square_next, got))
    with jax.named_scope("section_average"):
        back, mean = call(
            reduce_kernel, [VM] * 4, [((devices, 6, LANES), F32), ((PER, ROWS, LANES), F32)],
            [pltpu.VMEM((devices, LANES), F32)],
        )(got, upper_chunk, table, before)
    returned = lax.all_to_all(back, "scen", 0, 0, tiled=True)
    with jax.named_scope("selected"):
        early, late, second, pushed = call(
            select_kernel, [VM, FAR, FAR, VM, VM],
            [(slab, F32), (slab, F32), (field, F32), (field, F32)],
            [pltpu.VMEM(field, F32), pltpu.VMEM(field, F32), pltpu.SemaphoreType.DMA((2,))],
        )(returned, local, local_second, table, before)
    new_before = shifted(late, "per", 1)
    with jax.named_scope("push"):
        images, first, near = call(
            push_kernel, [VM] * 7 + [SM], [(field, F32), (slab, F32), (slab, F32)],
            scratch(2 * ROWS), 12,
        )(early, late, pushed, high, low, carry, table, code)
    far = shifted(first, "per", -1)
    with jax.named_scope("second_pull"):
        net, primal_new, early_probe, late_probe = call(
            second_kernel, [VM] * 14 + [SM],
            [(field, F32), (field, F32), (slab, F32), (slab, F32)],
            scratch(ROWS) + [pltpu.VMEM((PER * RB * ROWS, TILE), F32)], 8,
        )(early, late, new_before, images, second, near, far, mean, square_next, upper, carry,
          high, low, table, code)
    probe_before = shifted(late_probe, "per", 1)
    with jax.named_scope("second_push"):
        primal, partial = call(
            result_kernel, [VM] * 12 + [SM], [(dual_start.shape, F32), (dual_start.shape, F32)],
            scratch(ROWS) + [pltpu.VMEM(field, F32), pltpu.VMEM(field, F32)], 8,
        )(early_probe, late_probe, high, low, dual_start, demand, net, early, late, primal_new,
          carry, table, code)
    with jax.named_scope("correction"):
        (dual,) = call(correct_kernel, [VM] * 4, [(dual_start.shape, F32)], aliases={0: 0})(
            partial, probe_before, carry, table
        )
    return primal, dual


def solution(mesh):
    return jax.shard_map(
        per_device,
        mesh=mesh,
        in_specs=(
            P("scen", "per", None),
            P("scen", "per", None),
            P("per", None),
            P("per", None),
            P("per", None),
            P("scen"),
            P("per"),
            P("per", None, None),
            P("per", None, None),
            P(),
            P(),
            P(),
            P(None, "per"),
        ),
        out_specs=(P("scen", "per", None), P("scen", "per", None)),
        check_vma=False,
    )
```

```python
import jax
import jax.numpy as jnp
from jax import lax
from jax.experimental import pallas as pl
from jax.experimental.pallas import tpu as pltpu
from jax.sharding import PartitionSpec as P

TILE = 512
NPOOL = 3
NB = 3
SUBTREES = 8
RB = 16
LANES = 128
ROWS = 8
PER = 2
QUARTERS = TILE // LANES
MIB = 1 << 20
F32 = jnp.float32
BF16 = jnp.bfloat16

VM = pl.BlockSpec(memory_space=pltpu.VMEM)
SM = pl.BlockSpec(memory_space=pltpu.SMEM)
FAR = pl.BlockSpec(memory_space=pltpu.HBM)
PROB, RATE, DUAL_RATE, DAMP, FLAG, SECTION, PRODUCTS, TABLE = 0, 1, 2, 3, 5, 7, 9, 17


def shifted(block, axis, distance):
    devices = range(lax.axis_size(axis))
    route = [(i - distance, i) for i in devices if i - distance in devices]
    return lax.ppermute(block, axis, route)


def call(body, specs, outs, scratch=(), limit=4, places=None, work=0):
    return pl.pallas_call(
        body,
        out_shape=[jax.ShapeDtypeStruct(shape, dtype) for shape, dtype in outs],
        in_specs=specs,
        out_specs=places or [VM] * len(outs),
        scratch_shapes=list(scratch),
        cost_estimate=pl.CostEstimate(
            flops=work, bytes_accessed=work // 256, transcendentals=0
        ) if work else None,
        compiler_params=pltpu.CompilerParams(vmem_limit_bytes=limit * MIB),
    )


def lanes_of(ref, row, block):
    return ref[row : row + 1, block * TILE : (block + 1) * TILE]


def widened(column):
    return jnp.concatenate([column] * QUARTERS, axis=1)


def entry_of(table_ref, index):
    return widened(table_ref[index])


def group_sum(values, inside):
    row = lax.broadcasted_iota(jnp.int32, values.shape, 0)
    for step in (1, 2, 4):
        partner = jnp.where(
            (row & step) != 0,
            pltpu.roll(values, step, 0),
            pltpu.roll(values, ROWS - step, 0),
        )
        values = jnp.where(inside > step, values + partner, values)
    return values


def halves(values):
    high = values.astype(BF16)
    return high, (values - high.astype(F32)).astype(BF16)


def product_images(lhs_ref, high_ref, low_ref, image_ref, transposed, ready=None):
    rows = lhs_ref.shape[0]
    high, low = halves(lhs_ref[...])
    both = jnp.concatenate([high, low], axis=0)
    dims = (((1,), (0,)), ((), ())) if transposed else (((1,), (1,)), ((), ()))

    def dot(a, b):
        return lax.dot_general(a, b, dims, preferred_element_type=F32)

    for j in range(NPOOL):
        if ready is not None:
            ready(j)
        main = dot(both, high_ref[j])
        image_ref[j] = main[:rows] + main[rows:] + dot(high, low_ref[j])


def code_of(code_refs, period, block, k):
    return tuple(ref[k, period, block] for ref in code_refs)


def gathered_blocks(image_ref, code_refs, period, block, height):
    total = None
    for k in range(NB):
        which, place = code_of(code_refs, period, block, k)
        first = pl.multiple_of((period * RB + place) * height, height)
        part = image_ref[which, pl.ds(first, height), :]
        total = part if total is None else total + part
    return total


def scattered_blocks(image_ref, code_refs, out_ref, height):
    out_ref[...] = jnp.zeros_like(out_ref)
    for period in range(PER):
        for block in range(RB):
            first = (period * RB + block) * height
            for k in range(NB):
                which, column = code_of(code_refs, period, block, k)
                part = image_ref[which, first : first + height, :]
                place = pl.multiple_of((period * RB + column) * height, height)
                out_ref[pl.ds(place, height), :] += part


def fetch(pairs, sems):
    copies = [
        pltpu.make_async_copy(source, place, sems.at[i]) for i, (source, place) in enumerate(pairs)
    ]
    for copy in copies:
        copy.start()
    return copies


def carried_kernel(dual_hbm, demand_hbm, carry_hbm, prob_hbm, section_hbm, steps_hbm, subtree_hbm,
                   restart_hbm, carried_ref, late_ref, table_ref,
                   dual_ref, demand_ref, carry_ref, prob_ref, section_ref, steps_ref, subtree_ref,
                   restart_ref, first_ref, other_ref, sems):
    copies = fetch(
        [(prob_hbm, prob_ref), (section_hbm, section_ref), (steps_hbm, steps_ref),
         (subtree_hbm, subtree_ref), (restart_hbm, restart_ref), (carry_hbm, carry_ref),
         (dual_hbm, dual_ref), (demand_hbm, demand_ref)], sems)
    for copy in copies[:6]:
        copy.wait()
    device = lax.axis_index("scen")
    share = lax.axis_size("scen") // SUBTREES
    shape = (ROWS, LANES)
    row = lax.broadcasted_iota(jnp.int32, shape, 0)
    column = jnp.zeros(shape, F32)
    for s in range(ROWS):
        column = jnp.where(row == s, prob_ref[s], column)
    entry = subtree_ref[device // share]
    rate, dual_rate = steps_ref[0, entry], steps_ref[1, entry]
    table_ref[PROB] = column
    table_ref[RATE] = jnp.full(shape, rate)
    table_ref[DUAL_RATE] = jnp.full(shape, dual_rate)
    damps = []
    for period in range(PER):
        damps.append(jnp.where(restart_ref[0, period] == 1, 0.5, 1.0).astype(F32))
        table_ref[DAMP + period] = jnp.full(shape, damps[period])
        table_ref[FLAG + period] = jnp.full(shape, restart_ref[1, period].astype(F32))
        table_ref[SECTION + period] = jnp.full(shape, section_ref[period].astype(F32))
    assert share == ROWS
    for subtree in range(SUBTREES):
        other = subtree_ref[subtree]
        value = steps_ref[0, other] * steps_ref[1, other]
        table_ref[PRODUCTS + subtree] = jnp.full(shape, value)
    late_ref[...] = table_ref[SECTION + 1]
    for copy in copies[6:]:
        copy.wait()
    for s in range(ROWS):
        a, b = dual_ref[s, 0:1, :], demand_ref[s, 0:1, :]
        for block in range(RB):
            lanes = slice(block * TILE, (block + 1) * TILE)
            first_ref[block, s : s + 1, :] = a[:, lanes]
            other_ref[block, s : s + 1, :] = b[:, lanes]
    factor = damps[0] * dual_rate
    for block in range(RB):
        weight = lanes_of(carry_ref, 0, block)
        a = first_ref[block]
        carried_ref[block, 0:ROWS, :] = weight * a
        carried_ref[block, ROWS : 2 * ROWS, :] = weight * (a + factor * other_ref[block])


def pull_kernel(dual_hbm, demand_hbm, pool_hbm, carry_hbm, cost_hbm, cols_hbm, which_hbm, table_ref,
                raw_ref, high_hbm, low_hbm, dual_ref, demand_ref, pool_ref, carry_ref, cost_ref,
                cols_ref, which_ref, high_ref, low_ref, lhs_ref, image_ref, sems, out_sems):
    copies = fetch(
        [(dual_hbm, dual_ref), (demand_hbm, demand_ref)]
        + [(pool_hbm.at[j], pool_ref.at[j]) for j in range(NPOOL)]
        + [(carry_hbm, carry_ref), (cost_hbm, cost_ref), (cols_hbm, cols_ref),
           (which_hbm, which_ref)], sems)
    written = []
    copies[0].wait()
    copies[1].wait()
    for period in range(PER):
        factor = table_ref[DAMP + period, 0:1, 0:1] * table_ref[DUAL_RATE, 0:1, 0:1]
        for s in range(ROWS):
            a = dual_ref[s, period : period + 1, :]
            moved = a + factor * demand_ref[s, period : period + 1, :]
            for block in range(RB):
                lanes = slice(block * TILE, (block + 1) * TILE)
                first = (period * RB + block) * 2 * ROWS + s
                lhs_ref[first : first + 1, :] = a[:, lanes]
                lhs_ref[first + ROWS : first + ROWS + 1, :] = moved[:, lanes]

    def ready(j):
        copies[2 + j].wait()
        high, low = halves(pool_ref[j])
        high_ref[j] = high
        low_ref[j] = low
        for i, (source, out) in enumerate(((high_ref, high_hbm), (low_ref, low_hbm))):
            copy = pltpu.make_async_copy(source.at[j], out.at[j], out_sems.at[2 * j + i])
            copy.start()
            written.append(copy)

    product_images(lhs_ref, high_ref, low_ref, image_ref, True, ready)
    for copy in copies[5:]:
        copy.wait()
    scattered_blocks(image_ref, (which_ref, cols_ref), raw_ref, 2 * ROWS)
    rate = jnp.concatenate([entry_of(table_ref, RATE)] * 2, axis=0)
    for period in range(PER):
        for block in range(RB):
            first = (period * RB + block) * 2 * ROWS
            here = slice(first, first + 2 * ROWS)
            value = raw_ref[here, :] - lanes_of(cost_ref, period, block)
            if period == 0:
                later = (RB + block) * 2 * ROWS
                value -= lanes_of(carry_ref, 1, block) * lhs_ref[later : later + 2 * ROWS, :]
            raw_ref[here, :] = rate * value
    for copy in written:
        copy.wait()


def local_kernel(raw_ref, arriving_ref, upper_ref, table_ref, before_ref,
                 kept_ref, message_ref, chunk_ref):
    place = pl.multiple_of(lax.axis_index("scen") * LANES, LANES)
    chunk_ref[PER] = before_ref[...]
    rate = entry_of(table_ref, RATE)
    product = rate * entry_of(table_ref, DUAL_RATE)
    weight = entry_of(table_ref, PROB)
    mass = jnp.sum(weight, axis=0, keepdims=True)
    for period in range(PER):
        section = entry_of(table_ref, SECTION + period)
        inverse = 1.0 / group_sum(weight, section)
        wide = section[0:1] > ROWS
        for block in range(RB):
            first = (period * RB + block) * 2 * ROWS
            raw = raw_ref[first : first + ROWS, :]
            other = raw_ref[first + ROWS : first + 2 * ROWS, :]
            if period == 1:
                raw -= rate * arriving_ref[block, 0:ROWS, :]
                other -= rate * arriving_ref[block, ROWS : 2 * ROWS, :]
            averaged = group_sum(weight * raw, section) * inverse
            second = group_sum(weight * other, section) * inverse
            new = jnp.minimum(jnp.maximum(averaged, 0.0), lanes_of(upper_ref, period, block))
            kept_ref[0, period, block] = new
            kept_ref[1, period, block] = second
            pushed = jnp.sum(product * weight * new, axis=0, keepdims=True)
            sums = jnp.where(wide, mass * averaged[0:1], pushed)
            second_sums = mass * second[0:1]
            for quarter in range(QUARTERS):
                lanes = slice(quarter * LANES, (quarter + 1) * LANES)
                chunk = block * QUARTERS + quarter
                message_ref[chunk, period : period + 1, :] = sums[:, lanes]
                message_ref[chunk, 2 + period : 3 + period, :] = second_sums[:, lanes]
        chunk_ref[period] = jnp.broadcast_to(
            upper_ref[period : period + 1, pl.ds(place, LANES)], (ROWS, LANES)
        )
    for chunk in range(RB * QUARTERS):
        message_ref[chunk, 4:5, :] = mass[:, :LANES]


def reduce_kernel(got_ref, chunk_ref, table_ref, back_ref, mean_ref, moment_ref):
    devices = got_ref.shape[0]
    row = lax.broadcasted_iota(jnp.int32, (devices, devices), 0)
    column = lax.broadcasted_iota(jnp.int32, (devices, devices), 1)

    def member(section):
        span = jnp.maximum(section[0:1, 0:devices].astype(jnp.int32) // ROWS, 1)
        return ((row & -span) == (column & -span)).astype(F32)

    def dot(a, b):
        return jnp.dot(a, b, precision=lax.Precision.HIGHEST, preferred_element_type=F32)

    device = lax.axis_index("scen")
    mass = got_ref[:, 4, :]
    moment = mass * table_ref[PRODUCTS:TABLE].reshape(devices, LANES)
    befores = (chunk_ref[PER], table_ref[SECTION])
    for period in range(PER):
        section = table_ref[SECTION + period]
        same = member(section)
        inverse = 1.0 / dot(same, mass)
        sums = got_ref[:, period, :]
        upper = chunk_ref[period, 0:1, :]
        new = jnp.minimum(jnp.maximum(dot(same, sums) * inverse, 0.0), upper)
        back_ref[:, period, :] = new
        back_ref[:, 2 + period, :] = dot(same, got_ref[:, 2 + period, :]) * inverse
        moment_ref[...] = dot(same, moment) * inverse
        mean_ref[period] = jnp.broadcast_to(moment_ref[pl.ds(device, 1), :], (ROWS, LANES))
        source = jnp.where(section[0:1] > ROWS, moment * new, sums)
        same = member(befores[period])
        back_ref[:, 4 + period, :] = dot(same, source) / dot(same, mass)


def row_of(returned_ref, index, block):
    parts = [
        returned_ref[block * QUARTERS + quarter, index : index + 1, :] for quarter in range(QUARTERS)
    ]
    return jnp.concatenate(parts, axis=1)


def select_kernel(returned_ref, kept_ref, table_ref, chunk_ref,
                  early_ref, late_ref, second_ref, pushed_ref):
    product = entry_of(table_ref, RATE) * entry_of(table_ref, DUAL_RATE)
    weight = entry_of(table_ref, PROB)
    befores = (entry_of(chunk_ref, PER), entry_of(table_ref, SECTION))
    for period in range(PER):
        out_ref = (early_ref, late_ref)[period]
        wide = entry_of(table_ref, SECTION + period) > ROWS
        wide_before = befores[period] > ROWS
        scale = product / group_sum(weight, befores[period])
        for block in range(RB):
            shape = (ROWS, TILE)
            row = jnp.broadcast_to(row_of(returned_ref, period, block), shape)
            new = jnp.where(wide, row, kept_ref[0, period, block])
            out_ref[block] = new
            row = jnp.broadcast_to(row_of(returned_ref, 2 + period, block), shape)
            second_ref[period, block] = jnp.where(wide, row, kept_ref[1, period, block])
            row = jnp.broadcast_to(row_of(returned_ref, 4 + period, block), shape)
            averaged = scale * group_sum(weight * new, befores[period])
            pushed_ref[period, block] = jnp.where(wide_before, row, averaged)


def push_kernel(early_ref, late_ref, pushed_ref, high_ref, low_ref, carry_ref, table_ref,
                cols_hbm, which_hbm, image_out_ref, first_ref, next_ref, lhs_ref, image_ref,
                cols_ref, which_ref, sems):
    copies = fetch([(cols_hbm, cols_ref), (which_hbm, which_ref)], sems)
    code_refs = which_ref, cols_ref
    for period in range(PER):
        new_ref = (early_ref, late_ref)[period]
        for block in range(RB):
            first = (period * RB + block) * 2 * ROWS
            lhs_ref[first : first + ROWS, :] = new_ref[block]
            lhs_ref[first + ROWS : first + 2 * ROWS, :] = pushed_ref[period, block]
    product_images(lhs_ref, high_ref, low_ref, image_ref, False)
    for copy in copies:
        copy.wait()
    for period in range(PER):
        out_ref = (first_ref, next_ref)[period]
        factor = 2.0 * entry_of(table_ref, DAMP + period)
        for block in range(RB):
            both = gathered_blocks(image_ref, code_refs, period, block, 2 * ROWS)
            image_out_ref[period, block] = both[:ROWS]
            carry = lanes_of(carry_ref, period, block)
            out_ref[block] = factor * carry * both[ROWS:]
            if period == 0:
                row = block % ROWS
                out_ref[RB + block // ROWS, row : row + 1, :] = 0.5 * factor[0:1] * carry * carry


def second_kernel(early_ref, late_ref, before_ref, images_ref, second_ref, near_ref, far_ref,
                  mean_ref, upper_ref, carry_ref, high_ref, low_ref, table_ref, cols_hbm, which_hbm,
                  net_ref, primal_ref, early_probe_ref, late_probe_ref,
                  pulled_ref, lhs_ref, image_ref, cols_ref, which_ref, sems):
    copies = fetch([(cols_hbm, cols_ref), (which_hbm, which_ref)], sems)
    code_refs = which_ref, cols_ref
    for period in range(PER):
        previous_ref = (before_ref, early_ref)[period]
        factor = entry_of(table_ref, DAMP + period) * widened(mean_ref[period])
        for block in range(RB):
            carry = lanes_of(carry_ref, period, block)
            net = 2.0 * (images_ref[period, block] - carry * previous_ref[block])
            net_ref[period, block] = net
            first = (period * RB + block) * ROWS
            lhs_ref[first : first + ROWS, :] = factor * net
    product_images(lhs_ref, high_ref, low_ref, image_ref, True)
    for copy in copies:
        copy.wait()
    scattered_blocks(image_ref, code_refs, pulled_ref, ROWS)
    for period in range(PER):
        new_ref = (early_ref, late_ref)[period]
        next_ref = (near_ref, far_ref)[period]
        probe_ref = (early_probe_ref, late_probe_ref)[period]
        damp = entry_of(table_ref, DAMP + period)
        mean = 2.0 * widened(mean_ref[period])
        if period == 0:
            mean *= entry_of(table_ref, DAMP + 1)
        for block in range(RB):
            if period == 0:
                carry = lanes_of(carry_ref, 1, block)
                square = carry * carry
            else:
                row = block % ROWS
                square = far_ref[RB + block // ROWS, row : row + 1, :]
            first = (period * RB + block) * ROWS
            new = new_ref[block]
            primal = damp * new
            averaged = (
                primal + second_ref[period, block] - pulled_ref[first : first + ROWS, :]
                + next_ref[block] - square * mean * new
            )
            primal_new = jnp.minimum(jnp.maximum(averaged, 0.0), lanes_of(upper_ref, period, block))
            primal_ref[period, block] = primal_new
            probe_ref[block] = 2.0 * primal_new - primal


def result_kernel(early_probe_ref, late_probe_ref, high_ref, low_ref, dual_ref, demand_ref, net_ref,
                  early_ref, late_ref, new_ref, carry_ref, table_ref, cols_hbm, which_hbm,
                  primal_ref, out_ref, start_ref, target_ref, lhs_ref, image_ref,
                  cols_ref, which_ref, sems):
    copies = fetch([(cols_hbm, cols_ref), (which_hbm, which_ref)], sems)
    code_refs = which_ref, cols_ref
    for period in range(PER):
        probe_ref = (early_probe_ref, late_probe_ref)[period]
        for block in range(RB):
            first = (period * RB + block) * ROWS
            lhs_ref[first : first + ROWS, :] = probe_ref[block]
        for s in range(ROWS):
            a = dual_ref[s, period : period + 1, :]
            b = demand_ref[s, period : period + 1, :]
            for block in range(RB):
                lanes = slice(block * TILE, (block + 1) * TILE)
                start_ref[period, block, s : s + 1, :] = a[:, lanes]
                target_ref[period, block, s : s + 1, :] = b[:, lanes]
    product_images(lhs_ref, high_ref, low_ref, image_ref, False)
    for copy in copies:
        copy.wait()
    dual_rate = entry_of(table_ref, DUAL_RATE)
    for period in range(PER):
        first_ref = (early_ref, late_ref)[period]
        damp = entry_of(table_ref, DAMP + period)
        count = 2.0 * damp
        flagged = entry_of(table_ref, FLAG + period) == 1.0
        share = 1.0 / (count + 1.0)
        for block in range(RB):
            start, target = start_ref[period, block], target_ref[period, block]
            change = dual_rate * (target - net_ref[period, block])
            image = gathered_blocks(image_ref, code_refs, period, block, ROWS)
            if period == 1:
                image -= lanes_of(carry_ref, 1, block) * early_probe_ref[block]
            dual_new = start + damp * change + dual_rate * (target - image)
            dual_mean = (count * (start + 0.5 * change) + dual_new) * share
            primal_new = new_ref[period, block]
            primal_mean = (count * (0.5 * first_ref[block]) + primal_new) * share
            primal = jnp.where(flagged, primal_mean, primal_new)
            dual = jnp.where(flagged, dual_mean, dual_new)
            lanes = slice(block * TILE, (block + 1) * TILE)
            for s in range(ROWS):
                primal_ref[s, period : period + 1, lanes] = primal[s : s + 1]
                out_ref[s, period : period + 1, lanes] = dual[s : s + 1]


def correct_kernel(partial_ref, before_ref, carry_ref, table_ref, out_hbm, out_ref, added_ref, sems):
    share = 1.0 / (2.0 * entry_of(table_ref, DAMP) + 1.0)
    factor = entry_of(table_ref, DUAL_RATE) * jnp.where(
        entry_of(table_ref, FLAG) == 1.0, share, 1.0
    )
    for block in range(RB):
        added_ref[:, block * TILE : (block + 1) * TILE] = (
            factor * lanes_of(carry_ref, 0, block) * before_ref[block]
        )
    copies = []
    for s in range(ROWS):
        out_ref[s, 0:1, :] = partial_ref[s, 0:1, :] + added_ref[s : s + 1, :]
        out_ref[s, 1:2, :] = partial_ref[s, 1:2, :]
        copy = pltpu.make_async_copy(out_ref.at[s], out_hbm.at[s], sems.at[s])
        copy.start()
        copies.append(copy)
    for copy in copies:
        copy.wait()


def per_device(
    dual_start,
    demand,
    cost,
    upper,
    carry,
    prob,
    section_size,
    block_cols,
    block_pool,
    pool_tiles,
    step_table,
    subtree_step,
    restart,
):
    rows, periods, feature = dual_start.shape
    devices = lax.axis_size("scen")
    field = (PER, RB, ROWS, TILE)
    slab = (RB, ROWS, TILE)
    tiles = (NPOOL, TILE, TILE)
    packed = (PER, feature)

    def scratch(height):
        count = PER * RB * height
        return [pltpu.VMEM((count, TILE), F32), pltpu.VMEM((NPOOL, count, TILE), F32)]

    codes = (block_cols.transpose(2, 0, 1), block_pool.transpose(2, 0, 1))
    code_scratch = [
        pltpu.SMEM((NB, PER, RB), jnp.int32), pltpu.SMEM((NB, PER, RB), jnp.int32),
        pltpu.SemaphoreType.DMA((2,)),
    ]
    heavy = 2 * 3 * NPOOL * TILE * TILE * PER * RB * ROWS

    with jax.named_scope("carried"):
        carried, late_section, table = call(
            carried_kernel, [FAR] * 8,
            [((RB, 2 * ROWS, TILE), F32), ((ROWS, LANES), F32), ((TABLE, ROWS, LANES), F32)],
            [pltpu.VMEM(dual_start.shape, F32), pltpu.VMEM(dual_start.shape, F32),
             pltpu.VMEM(packed, F32), pltpu.SMEM((ROWS,), F32), pltpu.SMEM((PER,), jnp.int32),
             pltpu.SMEM(step_table.shape[::-1], F32), pltpu.SMEM((SUBTREES,), jnp.int32),
             pltpu.SMEM(restart.shape, jnp.int32), pltpu.VMEM(slab, F32), pltpu.VMEM(slab, F32),
             pltpu.SemaphoreType.DMA((8,))], 60,
        )(dual_start, demand, carry, prob, section_size, step_table.T, subtree_step, restart)
    arriving = shifted(carried, "per", -1)
    before = shifted(late_section, "per", 1)
    with jax.named_scope("first_pull"):
        raw, high, low = call(
            pull_kernel, [FAR] * 7 + [VM],
            [((PER * RB * 2 * ROWS, TILE), F32), (tiles, BF16), (tiles, BF16)],
            [pltpu.VMEM(dual_start.shape, F32), pltpu.VMEM(dual_start.shape, F32),
             pltpu.VMEM(tiles, F32), pltpu.VMEM(packed, F32), pltpu.VMEM(packed, F32),
             pltpu.SMEM((NB, PER, RB), jnp.int32), pltpu.SMEM((NB, PER, RB), jnp.int32),
             pltpu.VMEM(tiles, BF16), pltpu.VMEM(tiles, BF16)]
            + scratch(2 * ROWS) + [pltpu.SemaphoreType.DMA((9,)), pltpu.SemaphoreType.DMA((6,))],
            60, [VM, FAR, FAR], 2 * heavy,
        )(dual_start, demand, pool_tiles, carry, cost, *codes, table)
    with jax.named_scope("local_average"):
        kept, message, chunk = call(
            local_kernel, [VM] * 5,
            [((2,) + field, F32), ((devices, 5, LANES), F32), ((PER + 1, ROWS, LANES), F32)],
        )(raw, arriving, upper, table, before)
    got = lax.all_to_all(message, "scen", 0, 0, tiled=True)
    with jax.named_scope("section_average"):
        back, mean = call(
            reduce_kernel, [VM] * 3, [((devices, 6, LANES), F32), ((PER, ROWS, LANES), F32)],
            [pltpu.VMEM((devices, LANES), F32)],
        )(got, chunk, table)
    returned = lax.all_to_all(back, "scen", 0, 0, tiled=True)
    with jax.named_scope("selected"):
        early, late, second, pushed = call(
            select_kernel, [VM] * 4, [(slab, F32), (slab, F32), (field, F32), (field, F32)],
        )(returned, kept, table, chunk)
    new_before = shifted(late, "per", 1)
    with jax.named_scope("push"):
        images, first, near = call(
            push_kernel, [VM] * 7 + [FAR] * 2,
            [(field, F32), ((RB + RB // ROWS, ROWS, TILE), F32), (slab, F32)],
            scratch(2 * ROWS) + code_scratch, 12, work=2 * heavy,
        )(early, late, pushed, high, low, carry, table, *codes)
    new_before, first = lax.optimization_barrier((new_before, first))
    far = shifted(first, "per", -1)
    with jax.named_scope("second_pull"):
        net, primal_new, early_probe, late_probe = call(
            second_kernel, [VM] * 13 + [FAR] * 2,
            [(field, F32), (field, F32), (slab, F32), (slab, F32)],
            [pltpu.VMEM((PER * RB * ROWS, TILE), F32)] + scratch(ROWS) + code_scratch, 8, work=heavy,
        )(early, late, new_before, images, second, near, far, mean, upper, carry,
          high, low, table, *codes)
    probe_before = shifted(late_probe, "per", 1)
    with jax.named_scope("second_push"):
        primal, partial = call(
            result_kernel, [VM] * 12 + [FAR] * 2, [(dual_start.shape, F32), (dual_start.shape, F32)],
            [pltpu.VMEM(field, F32), pltpu.VMEM(field, F32)] + scratch(ROWS) + code_scratch, 8,
            work=heavy,
        )(early_probe, late_probe, high, low, dual_start, demand, net, early, late, primal_new,
          carry, table, *codes)
    with jax.named_scope("correction"):
        (dual,) = call(
            correct_kernel, [VM] * 4, [(dual_start.shape, F32)],
            [pltpu.VMEM(dual_start.shape, F32), pltpu.VMEM((ROWS, feature), F32),
             pltpu.SemaphoreType.DMA((ROWS,))], places=[FAR],
        )(partial, probe_before, carry, table)
    return primal, dual


def solution(mesh):
    return jax.shard_map(
        per_device,
        mesh=mesh,
        in_specs=(
            P("scen", "per", None),
            P("scen", "per", None),
            P("per", None),
            P("per", None),
            P("per", None),
            P("scen"),
            P("per"),
            P("per", None, None),
            P("per", None, None),
            P(),
            P(),
            P(),
            P(None, "per"),
        ),
        out_specs=(P("scen", "per", None), P("scen", "per", None)),
        check_vma=False,
    )
```

```python
import jax
import jax.numpy as jnp
from jax import lax
from jax.experimental import pallas as pl
from jax.experimental.pallas import tpu as pltpu
from jax.sharding import PartitionSpec as P

TILE = 512
NPOOL = 3
NB = 3
SUBTREES = 8
RB = 16
LANES = 128
ROWS = 8
PER = 2
QUARTERS = TILE // LANES
MIB = 1 << 20
F32 = jnp.float32
BF16 = jnp.bfloat16

VM = pl.BlockSpec(memory_space=pltpu.VMEM)
SM = pl.BlockSpec(memory_space=pltpu.SMEM)
FAR = pl.BlockSpec(memory_space=pltpu.HBM)
PROB, RATE, DUAL_RATE, DAMP, FLAG, SECTION, PRODUCTS, TABLE = 0, 1, 2, 3, 5, 7, 9, 17


def shifted(block, axis, distance):
    devices = range(lax.axis_size(axis))
    route = [(i - distance, i) for i in devices if i - distance in devices]
    return lax.ppermute(block, axis, route)


def call(body, specs, outs, scratch=(), limit=4, places=None, work=0):
    return pl.pallas_call(
        body,
        out_shape=[jax.ShapeDtypeStruct(shape, dtype) for shape, dtype in outs],
        in_specs=specs,
        out_specs=places or [VM] * len(outs),
        scratch_shapes=list(scratch),
        cost_estimate=pl.CostEstimate(
            flops=work, bytes_accessed=work // 256, transcendentals=0
        ) if work else None,
        compiler_params=pltpu.CompilerParams(vmem_limit_bytes=limit * MIB),
    )


def lanes_of(ref, row, block):
    return ref[row : row + 1, block * TILE : (block + 1) * TILE]


def widened(column):
    return jnp.concatenate([column] * QUARTERS, axis=1)


def entry_of(table_ref, index):
    return widened(table_ref[index])


def group_sum(values, inside):
    row = lax.broadcasted_iota(jnp.int32, values.shape, 0)
    for step in (1, 2, 4):
        partner = jnp.where(
            (row & step) != 0,
            pltpu.roll(values, step, 0),
            pltpu.roll(values, ROWS - step, 0),
        )
        values = jnp.where(inside > step, values + partner, values)
    return values


def halves(values):
    high = values.astype(BF16)
    return high, (values - high.astype(F32)).astype(BF16)


def product_images(lhs_ref, high_ref, low_ref, image_ref, transposed, ready=None):
    rows = lhs_ref.shape[0]
    high, low = halves(lhs_ref[...])
    both = jnp.concatenate([high, low], axis=0)
    dims = (((1,), (0,)), ((), ())) if transposed else (((1,), (1,)), ((), ()))

    def dot(a, b):
        return lax.dot_general(a, b, dims, preferred_element_type=F32)

    for j in range(NPOOL):
        if ready is not None:
            ready(j)
        main = dot(both, high_ref[j])
        image_ref[j] = main[:rows] + main[rows:] + dot(high, low_ref[j])


def code_of(code_refs, period, block, k):
    return tuple(ref[k, period, block] for ref in code_refs)


def gathered_blocks(image_ref, code_refs, period, block, height, slot):
    total = None
    for k in range(NB):
        which, place = code_of(code_refs, period, block, k)
        first = pl.multiple_of((slot * RB + place) * height, height)
        part = image_ref[which, pl.ds(first, height), :]
        total = part if total is None else total + part
    return total


def scattered_blocks(image_ref, code_refs, out_ref, height):
    out_ref[...] = jnp.zeros_like(out_ref)
    for period in range(PER):
        for block in range(RB):
            first = (period * RB + block) * height
            for k in range(NB):
                which, column = code_of(code_refs, period, block, k)
                part = image_ref[which, first : first + height, :]
                place = pl.multiple_of((period * RB + column) * height, height)
                out_ref[pl.ds(place, height), :] += part


def fetch(pairs, sems):
    copies = [
        pltpu.make_async_copy(source, place, sems.at[i]) for i, (source, place) in enumerate(pairs)
    ]
    for copy in copies:
        copy.start()
    return copies


def carried_kernel(dual_hbm, demand_hbm, carry_hbm, prob_hbm, section_hbm, steps_hbm, subtree_hbm,
                   restart_hbm, carried_ref, late_ref, table_ref,
                   dual_ref, demand_ref, carry_ref, prob_ref, section_ref, steps_ref, subtree_ref,
                   restart_ref, first_ref, other_ref, sems):
    copies = fetch(
        [(prob_hbm, prob_ref), (section_hbm, section_ref), (steps_hbm, steps_ref),
         (subtree_hbm, subtree_ref), (restart_hbm, restart_ref), (carry_hbm, carry_ref),
         (dual_hbm, dual_ref), (demand_hbm, demand_ref)], sems)
    for copy in copies[:6]:
        copy.wait()
    device = lax.axis_index("scen")
    share = lax.axis_size("scen") // SUBTREES
    shape = (ROWS, LANES)
    row = lax.broadcasted_iota(jnp.int32, shape, 0)
    column = jnp.zeros(shape, F32)
    for s in range(ROWS):
        column = jnp.where(row == s, prob_ref[s], column)
    entry = subtree_ref[device // share]
    rate, dual_rate = steps_ref[0, entry], steps_ref[1, entry]
    table_ref[PROB] = column
    table_ref[RATE] = jnp.full(shape, rate)
    table_ref[DUAL_RATE] = jnp.full(shape, dual_rate)
    damps = []
    for period in range(PER):
        damps.append(jnp.where(restart_ref[0, period] == 1, 0.5, 1.0).astype(F32))
        table_ref[DAMP + period] = jnp.full(shape, damps[period])
        table_ref[FLAG + period] = jnp.full(shape, restart_ref[1, period].astype(F32))
        table_ref[SECTION + period] = jnp.full(shape, section_ref[period].astype(F32))
    assert share == ROWS
    for subtree in range(SUBTREES):
        other = subtree_ref[subtree]
        value = steps_ref[0, other] * steps_ref[1, other]
        table_ref[PRODUCTS + subtree] = jnp.full(shape, value)
    late_ref[...] = table_ref[SECTION + 1]
    for copy in copies[6:]:
        copy.wait()
    for s in range(ROWS):
        a, b = dual_ref[s, 0:1, :], demand_ref[s, 0:1, :]
        for block in range(RB):
            lanes = slice(block * TILE, (block + 1) * TILE)
            first_ref[block, s : s + 1, :] = a[:, lanes]
            other_ref[block, s : s + 1, :] = b[:, lanes]
    factor = damps[0] * dual_rate
    for block in range(RB):
        weight = lanes_of(carry_ref, 0, block)
        a = first_ref[block]
        carried_ref[block, 0:ROWS, :] = weight * a
        carried_ref[block, ROWS : 2 * ROWS, :] = weight * (a + factor * other_ref[block])


def pull_kernel(dual_hbm, demand_hbm, pool_hbm, carry_hbm, cost_hbm, cols_hbm, which_hbm, table_ref,
                raw_ref, high_hbm, low_hbm, dual_ref, demand_ref, pool_ref, carry_ref, cost_ref,
                cols_ref, which_ref, high_ref, low_ref, lhs_ref, image_ref, sems, out_sems):
    copies = fetch(
        [(dual_hbm, dual_ref), (demand_hbm, demand_ref)]
        + [(pool_hbm.at[j], pool_ref.at[j]) for j in range(NPOOL)]
        + [(carry_hbm, carry_ref), (cost_hbm, cost_ref), (cols_hbm, cols_ref),
           (which_hbm, which_ref)], sems)
    written = []
    copies[0].wait()
    copies[1].wait()
    for period in range(PER):
        factor = table_ref[DAMP + period, 0:1, 0:1] * table_ref[DUAL_RATE, 0:1, 0:1]
        for s in range(ROWS):
            a = dual_ref[s, period : period + 1, :]
            moved = a + factor * demand_ref[s, period : period + 1, :]
            for block in range(RB):
                lanes = slice(block * TILE, (block + 1) * TILE)
                first = (period * RB + block) * 2 * ROWS + s
                lhs_ref[first : first + 1, :] = a[:, lanes]
                lhs_ref[first + ROWS : first + ROWS + 1, :] = moved[:, lanes]

    def ready(j):
        copies[2 + j].wait()
        high, low = halves(pool_ref[j])
        high_ref[j] = high
        low_ref[j] = low
        for i, (source, out) in enumerate(((high_ref, high_hbm), (low_ref, low_hbm))):
            copy = pltpu.make_async_copy(source.at[j], out.at[j], out_sems.at[2 * j + i])
            copy.start()
            written.append(copy)

    product_images(lhs_ref, high_ref, low_ref, image_ref, True, ready)
    for copy in copies[5:]:
        copy.wait()
    scattered_blocks(image_ref, (which_ref, cols_ref), raw_ref, 2 * ROWS)
    rate = jnp.concatenate([entry_of(table_ref, RATE)] * 2, axis=0)
    for period in range(PER):
        for block in range(RB):
            first = (period * RB + block) * 2 * ROWS
            here = slice(first, first + 2 * ROWS)
            value = raw_ref[here, :] - lanes_of(cost_ref, period, block)
            if period == 0:
                later = (RB + block) * 2 * ROWS
                value -= lanes_of(carry_ref, 1, block) * lhs_ref[later : later + 2 * ROWS, :]
            raw_ref[here, :] = rate * value
    for copy in written:
        copy.wait()


def local_kernel(raw_ref, arriving_ref, upper_ref, table_ref, before_ref,
                 kept_ref, message_ref, chunk_ref):
    place = pl.multiple_of(lax.axis_index("scen") * LANES, LANES)
    chunk_ref[PER] = before_ref[...]
    rate = entry_of(table_ref, RATE)
    product = rate * entry_of(table_ref, DUAL_RATE)
    weight = entry_of(table_ref, PROB)
    mass = jnp.sum(weight, axis=0, keepdims=True)
    for period in range(PER):
        section = entry_of(table_ref, SECTION + period)
        inverse = 1.0 / group_sum(weight, section)
        wide = section[0:1] > ROWS
        for block in range(RB):
            first = (period * RB + block) * 2 * ROWS
            raw = raw_ref[first : first + ROWS, :]
            other = raw_ref[first + ROWS : first + 2 * ROWS, :]
            if period == 1:
                raw -= rate * arriving_ref[block, 0:ROWS, :]
                other -= rate * arriving_ref[block, ROWS : 2 * ROWS, :]
            averaged = group_sum(weight * raw, section) * inverse
            second = group_sum(weight * other, section) * inverse
            new = jnp.minimum(jnp.maximum(averaged, 0.0), lanes_of(upper_ref, period, block))
            kept_ref[0, period, block] = new
            kept_ref[1, period, block] = second
            pushed = jnp.sum(product * weight * new, axis=0, keepdims=True)
            sums = jnp.where(wide, mass * averaged[0:1], pushed)
            second_sums = mass * second[0:1]
            for quarter in range(QUARTERS):
                lanes = slice(quarter * LANES, (quarter + 1) * LANES)
                chunk = block * QUARTERS + quarter
                message_ref[chunk, :, part_of(period)] = sums[:, lanes]
                message_ref[chunk, :, part_of(2 + period)] = second_sums[:, lanes]
        chunk_ref[period] = jnp.broadcast_to(
            upper_ref[period : period + 1, pl.ds(place, LANES)], (ROWS, LANES)
        )
    for chunk in range(RB * QUARTERS):
        message_ref[chunk, :, part_of(4)] = mass[:, :LANES]


def part_of(index):
    return slice(index * LANES, (index + 1) * LANES)


def reduce_kernel(got_ref, chunk_ref, table_ref, back_ref, mean_ref, moment_ref):
    devices = got_ref.shape[0]
    row = lax.broadcasted_iota(jnp.int32, (devices, devices), 0)
    column = lax.broadcasted_iota(jnp.int32, (devices, devices), 1)

    def member(section):
        span = jnp.maximum(section[0:1, 0:devices].astype(jnp.int32) // ROWS, 1)
        return ((row & -span) == (column & -span)).astype(F32)

    def dot(a, b):
        return jnp.dot(a, b, precision=lax.Precision.HIGHEST, preferred_element_type=F32)

    device = lax.axis_index("scen")
    mass = got_ref[:, 0, part_of(4)]
    moment = mass * table_ref[PRODUCTS:TABLE].reshape(devices, LANES)
    befores = (chunk_ref[PER], table_ref[SECTION])
    for period in range(PER):
        section = table_ref[SECTION + period]
        same = member(section)
        inverse = 1.0 / dot(same, mass)
        sums = got_ref[:, 0, part_of(period)]
        upper = chunk_ref[period, 0:1, :]
        new = jnp.minimum(jnp.maximum(dot(same, sums) * inverse, 0.0), upper)
        back_ref[:, 0, part_of(period)] = new
        back_ref[:, 0, part_of(2 + period)] = dot(same, got_ref[:, 0, part_of(2 + period)]) * inverse
        moment_ref[...] = dot(same, moment) * inverse
        mean_ref[period] = jnp.broadcast_to(moment_ref[pl.ds(device, 1), :], (ROWS, LANES))
        source = jnp.where(section[0:1] > ROWS, moment * new, sums)
        same = member(befores[period])
        back_ref[:, 0, part_of(4 + period)] = dot(same, source) / dot(same, mass)


def row_of(returned_ref, index, block):
    parts = [
        returned_ref[block * QUARTERS + quarter, :, part_of(index)] for quarter in range(QUARTERS)
    ]
    return jnp.concatenate(parts, axis=1)


def select_kernel(returned_ref, kept_ref, table_ref, chunk_ref,
                  early_ref, late_ref, second_ref, pushed_first_ref, pushed_next_ref):
    product = entry_of(table_ref, RATE) * entry_of(table_ref, DUAL_RATE)
    weight = entry_of(table_ref, PROB)
    befores = (entry_of(chunk_ref, PER), entry_of(table_ref, SECTION))
    for period in range(PER):
        out_ref = (early_ref, late_ref)[period]
        pushed_ref = (pushed_first_ref, pushed_next_ref)[period]
        wide = entry_of(table_ref, SECTION + period) > ROWS
        wide_before = befores[period] > ROWS
        scale = product / group_sum(weight, befores[period])
        for block in range(RB):
            shape = (ROWS, TILE)
            row = jnp.broadcast_to(row_of(returned_ref, period, block), shape)
            new = jnp.where(wide, row, kept_ref[0, period, block])
            out_ref[block] = new
            row = jnp.broadcast_to(row_of(returned_ref, 2 + period, block), shape)
            second_ref[period, block] = jnp.where(wide, row, kept_ref[1, period, block])
            row = jnp.broadcast_to(row_of(returned_ref, 4 + period, block), shape)
            averaged = scale * group_sum(weight * new, befores[period])
            pushed_ref[block] = jnp.where(wide_before, row, averaged)


def push_first_kernel(pushed_ref, high_ref, low_ref, carry_ref, table_ref, cols_hbm, which_hbm,
                      first_ref, lhs_ref, image_ref, cols_ref, which_ref, sems):
    copies = fetch([(cols_hbm, cols_ref), (which_hbm, which_ref)], sems)
    code_refs = which_ref, cols_ref
    for block in range(RB):
        lhs_ref[block * ROWS : (block + 1) * ROWS, :] = pushed_ref[block]
    product_images(lhs_ref, high_ref, low_ref, image_ref, False)
    for copy in copies:
        copy.wait()
    factor = 2.0 * entry_of(table_ref, DAMP)
    for block in range(RB):
        carry = lanes_of(carry_ref, 0, block)
        image = gathered_blocks(image_ref, code_refs, 0, block, ROWS, 0)
        first_ref[block] = factor * carry * image
        row = block % ROWS
        first_ref[RB + block // ROWS, row : row + 1, :] = 0.5 * factor[0:1] * carry * carry


def push_kernel(early_ref, late_ref, pushed_ref, high_ref, low_ref, carry_ref, table_ref,
                cols_hbm, which_hbm, image_out_ref, next_ref, lhs_ref, image_ref,
                cols_ref, which_ref, sems):
    copies = fetch([(cols_hbm, cols_ref), (which_hbm, which_ref)], sems)
    code_refs = which_ref, cols_ref
    for slot, field_ref in enumerate((early_ref, late_ref, pushed_ref)):
        for block in range(RB):
            first = (slot * RB + block) * ROWS
            lhs_ref[first : first + ROWS, :] = field_ref[block]
    product_images(lhs_ref, high_ref, low_ref, image_ref, False)
    for copy in copies:
        copy.wait()
    factor = 2.0 * entry_of(table_ref, DAMP + 1)
    for block in range(RB):
        for period in range(PER):
            image_out_ref[period, block] = gathered_blocks(
                image_ref, code_refs, period, block, ROWS, period
            )
        image = gathered_blocks(image_ref, code_refs, 1, block, ROWS, 2)
        next_ref[block] = factor * lanes_of(carry_ref, 1, block) * image


def net_kernel(early_ref, before_ref, images_ref, mean_ref, carry_ref, high_ref, low_ref, table_ref,
               cols_hbm, which_hbm, net_ref, pulled_ref, lhs_ref, image_ref,
               cols_ref, which_ref, sems):
    copies = fetch([(cols_hbm, cols_ref), (which_hbm, which_ref)], sems)
    code_refs = which_ref, cols_ref
    for period in range(PER):
        previous_ref = (before_ref, early_ref)[period]
        factor = entry_of(table_ref, DAMP + period) * widened(mean_ref[period])
        for block in range(RB):
            carry = lanes_of(carry_ref, period, block)
            net = 2.0 * (images_ref[period, block] - carry * previous_ref[block])
            net_ref[period, block] = net
            first = (period * RB + block) * ROWS
            lhs_ref[first : first + ROWS, :] = factor * net
    product_images(lhs_ref, high_ref, low_ref, image_ref, True)
    for copy in copies:
        copy.wait()
    scattered_blocks(image_ref, code_refs, pulled_ref, ROWS)


def primal_kernel(early_ref, late_ref, pulled_ref, second_ref, near_ref, far_ref, mean_ref,
                  upper_ref, carry_ref, table_ref, primal_ref, early_probe_ref, late_probe_ref):
    for period in range(PER):
        new_ref = (early_ref, late_ref)[period]
        next_ref = (near_ref, far_ref)[period]
        probe_ref = (early_probe_ref, late_probe_ref)[period]
        damp = entry_of(table_ref, DAMP + period)
        mean = 2.0 * widened(mean_ref[period])
        if period == 0:
            mean *= entry_of(table_ref, DAMP + 1)
        for block in range(RB):
            if period == 0:
                carry = lanes_of(carry_ref, 1, block)
                square = carry * carry
            else:
                row = block % ROWS
                square = far_ref[RB + block // ROWS, row : row + 1, :]
            first = (period * RB + block) * ROWS
            new = new_ref[block]
            primal = damp * new
            averaged = (
                primal + second_ref[period, block] - pulled_ref[first : first + ROWS, :]
                + next_ref[block] - square * mean * new
            )
            primal_new = jnp.minimum(jnp.maximum(averaged, 0.0), lanes_of(upper_ref, period, block))
            primal_ref[period, block] = primal_new
            probe_ref[block] = 2.0 * primal_new - primal


def result_kernel(early_probe_ref, late_probe_ref, high_ref, low_ref, dual_ref, demand_ref, net_ref,
                  early_ref, late_ref, new_ref, carry_ref, table_ref, cols_hbm, which_hbm,
                  primal_ref, out_ref, start_ref, target_ref, lhs_ref, image_ref,
                  cols_ref, which_ref, sems):
    copies = fetch([(cols_hbm, cols_ref), (which_hbm, which_ref)], sems)
    code_refs = which_ref, cols_ref
    for period in range(PER):
        probe_ref = (early_probe_ref, late_probe_ref)[period]
        for block in range(RB):
            first = (period * RB + block) * ROWS
            lhs_ref[first : first + ROWS, :] = probe_ref[block]
        for s in range(ROWS):
            a = dual_ref[s, period : period + 1, :]
            b = demand_ref[s, period : period + 1, :]
            for block in range(RB):
                lanes = slice(block * TILE, (block + 1) * TILE)
                start_ref[period, block, s : s + 1, :] = a[:, lanes]
                target_ref[period, block, s : s + 1, :] = b[:, lanes]
    product_images(lhs_ref, high_ref, low_ref, image_ref, False)
    for copy in copies:
        copy.wait()
    dual_rate = entry_of(table_ref, DUAL_RATE)
    for period in range(PER):
        first_ref = (early_ref, late_ref)[period]
        damp = entry_of(table_ref, DAMP + period)
        count = 2.0 * damp
        flagged = entry_of(table_ref, FLAG + period) == 1.0
        share = 1.0 / (count + 1.0)
        for block in range(RB):
            start, target = start_ref[period, block], target_ref[period, block]
            change = dual_rate * (target - net_ref[period, block])
            image = gathered_blocks(image_ref, code_refs, period, block, ROWS, period)
            if period == 1:
                image -= lanes_of(carry_ref, 1, block) * early_probe_ref[block]
            dual_new = start + damp * change + dual_rate * (target - image)
            dual_mean = (count * (start + 0.5 * change) + dual_new) * share
            primal_new = new_ref[period, block]
            primal_mean = (count * (0.5 * first_ref[block]) + primal_new) * share
            primal = jnp.where(flagged, primal_mean, primal_new)
            dual = jnp.where(flagged, dual_mean, dual_new)
            lanes = slice(block * TILE, (block + 1) * TILE)
            for s in range(ROWS):
                primal_ref[s, period : period + 1, lanes] = primal[s : s + 1]
                out_ref[s, period : period + 1, lanes] = dual[s : s + 1]


def correct_kernel(partial_ref, before_ref, carry_ref, table_ref, out_hbm, out_ref, added_ref, sems):
    share = 1.0 / (2.0 * entry_of(table_ref, DAMP) + 1.0)
    factor = entry_of(table_ref, DUAL_RATE) * jnp.where(
        entry_of(table_ref, FLAG) == 1.0, share, 1.0
    )
    for block in range(RB):
        added_ref[:, block * TILE : (block + 1) * TILE] = (
            factor * lanes_of(carry_ref, 0, block) * before_ref[block]
        )
    copies = []
    for s in range(ROWS):
        out_ref[s, 0:1, :] = partial_ref[s, 0:1, :] + added_ref[s : s + 1, :]
        out_ref[s, 1:2, :] = partial_ref[s, 1:2, :]
        copy = pltpu.make_async_copy(out_ref.at[s], out_hbm.at[s], sems.at[s])
        copy.start()
        copies.append(copy)
    for copy in copies:
        copy.wait()


def per_device(
    dual_start,
    demand,
    cost,
    upper,
    carry,
    prob,
    section_size,
    block_cols,
    block_pool,
    pool_tiles,
    step_table,
    subtree_step,
    restart,
):
    rows, periods, feature = dual_start.shape
    devices = lax.axis_size("scen")
    field = (PER, RB, ROWS, TILE)
    slab = (RB, ROWS, TILE)
    tiles = (NPOOL, TILE, TILE)
    packed = (PER, feature)

    def scratch(height, slots=PER):
        count = slots * RB * height
        return [pltpu.VMEM((count, TILE), F32), pltpu.VMEM((NPOOL, count, TILE), F32)]

    codes = (block_cols.transpose(2, 0, 1), block_pool.transpose(2, 0, 1))
    code_scratch = [
        pltpu.SMEM((NB, PER, RB), jnp.int32), pltpu.SMEM((NB, PER, RB), jnp.int32),
        pltpu.SemaphoreType.DMA((2,)),
    ]
    heavy = 2 * 3 * NPOOL * TILE * TILE * PER * RB * ROWS

    with jax.named_scope("carried"):
        carried, late_section, table = call(
            carried_kernel, [FAR] * 8,
            [((RB, 2 * ROWS, TILE), F32), ((ROWS, LANES), F32), ((TABLE, ROWS, LANES), F32)],
            [pltpu.VMEM(dual_start.shape, F32), pltpu.VMEM(dual_start.shape, F32),
             pltpu.VMEM(packed, F32), pltpu.SMEM((ROWS,), F32), pltpu.SMEM((PER,), jnp.int32),
             pltpu.SMEM(step_table.shape[::-1], F32), pltpu.SMEM((SUBTREES,), jnp.int32),
             pltpu.SMEM(restart.shape, jnp.int32), pltpu.VMEM(slab, F32), pltpu.VMEM(slab, F32),
             pltpu.SemaphoreType.DMA((8,))], 60,
        )(dual_start, demand, carry, prob, section_size, step_table.T, subtree_step, restart)
    arriving = shifted(carried, "per", -1)
    before = shifted(late_section, "per", 1)
    with jax.named_scope("first_pull"):
        raw, high, low = call(
            pull_kernel, [FAR] * 7 + [VM],
            [((PER * RB * 2 * ROWS, TILE), F32), (tiles, BF16), (tiles, BF16)],
            [pltpu.VMEM(dual_start.shape, F32), pltpu.VMEM(dual_start.shape, F32),
             pltpu.VMEM(tiles, F32), pltpu.VMEM(packed, F32), pltpu.VMEM(packed, F32),
             pltpu.SMEM((NB, PER, RB), jnp.int32), pltpu.SMEM((NB, PER, RB), jnp.int32),
             pltpu.VMEM(tiles, BF16), pltpu.VMEM(tiles, BF16)]
            + scratch(2 * ROWS) + [pltpu.SemaphoreType.DMA((9,)), pltpu.SemaphoreType.DMA((6,))],
            60, [VM, FAR, FAR], 2 * heavy,
        )(dual_start, demand, pool_tiles, carry, cost, *codes, table)
    with jax.named_scope("local_average"):
        kept, message, chunk = call(
            local_kernel, [VM] * 5,
            [((2,) + field, F32), ((devices, 1, 5 * LANES), F32), ((PER + 1, ROWS, LANES), F32)],
        )(raw, arriving, upper, table, before)
    got = lax.all_to_all(message, "scen", 0, 0, tiled=True)
    with jax.named_scope("section_average"):
        back, mean = call(
            reduce_kernel, [VM] * 3, [((devices, 1, 6 * LANES), F32), ((PER, ROWS, LANES), F32)],
            [pltpu.VMEM((devices, LANES), F32)],
        )(got, chunk, table)
    returned = lax.all_to_all(back, "scen", 0, 0, tiled=True)
    with jax.named_scope("selected"):
        early, late, second, pushed_first, pushed_next = call(
            select_kernel, [VM] * 4,
            [(slab, F32), (slab, F32), (field, F32), (slab, F32), (slab, F32)],
        )(returned, kept, table, chunk)
    new_before = shifted(late, "per", 1)
    with jax.named_scope("push_first"):
        (first,) = call(
            push_first_kernel, [VM] * 5 + [FAR] * 2, [((RB + RB // ROWS, ROWS, TILE), F32)],
            scratch(ROWS, 1) + code_scratch, 6, work=heavy // 2,
        )(pushed_first, high, low, carry, table, *codes)
    far = shifted(first, "per", -1)
    early, late, pushed_next, first = lax.optimization_barrier((early, late, pushed_next, first))
    with jax.named_scope("push"):
        images, near = call(
            push_kernel, [VM] * 7 + [FAR] * 2, [(field, F32), (slab, F32)],
            scratch(ROWS, 3) + code_scratch, 10, work=2 * heavy,
        )(early, late, pushed_next, high, low, carry, table, *codes)
    with jax.named_scope("second_pull"):
        net, pulled = call(
            net_kernel, [VM] * 8 + [FAR] * 2, [(field, F32), ((PER * RB * ROWS, TILE), F32)],
            scratch(ROWS) + code_scratch, 8, work=heavy,
        )(early, new_before, images, mean, carry, high, low, table, *codes)
    far, pulled = lax.optimization_barrier((far, pulled))
    with jax.named_scope("second_primal"):
        primal_new, early_probe, late_probe = call(
            primal_kernel, [VM] * 10, [(field, F32), (slab, F32), (slab, F32)],
        )(early, late, pulled, second, near, far, mean, upper, carry, table)
    probe_before = shifted(late_probe, "per", 1)
    with jax.named_scope("second_push"):
        primal, partial = call(
            result_kernel, [VM] * 12 + [FAR] * 2, [(dual_start.shape, F32), (dual_start.shape, F32)],
            [pltpu.VMEM(field, F32), pltpu.VMEM(field, F32)] + scratch(ROWS) + code_scratch, 8,
            work=heavy,
        )(early_probe, late_probe, high, low, dual_start, demand, net, early, late, primal_new,
          carry, table, *codes)
    with jax.named_scope("correction"):
        (dual,) = call(
            correct_kernel, [VM] * 4, [(dual_start.shape, F32)],
            [pltpu.VMEM(dual_start.shape, F32), pltpu.VMEM((ROWS, feature), F32),
             pltpu.SemaphoreType.DMA((ROWS,))], places=[FAR],
        )(partial, probe_before, carry, table)
    return primal, dual


def solution(mesh):
    return jax.shard_map(
        per_device,
        mesh=mesh,
        in_specs=(
            P("scen", "per", None),
            P("scen", "per", None),
            P("per", None),
            P("per", None),
            P("per", None),
            P("scen"),
            P("per"),
            P("per", None, None),
            P("per", None, None),
            P(),
            P(),
            P(),
            P(None, "per"),
        ),
        out_specs=(P("scen", "per", None), P("scen", "per", None)),
        check_vma=False,
    )
```

```python
import jax
import jax.numpy as jnp
from jax import lax
from jax.experimental import pallas as pl
from jax.experimental.pallas import tpu as pltpu
from jax.sharding import PartitionSpec as P

TILE = 512
NPOOL = 3
NB = 3
SUBTREES = 8
RB = 16
LANES = 128
ROWS = 8
PER = 2
QUARTERS = TILE // LANES
MIB = 1 << 20
F32 = jnp.float32
BF16 = jnp.bfloat16

VM = pl.BlockSpec(memory_space=pltpu.VMEM)
SM = pl.BlockSpec(memory_space=pltpu.SMEM)
FAR = pl.BlockSpec(memory_space=pltpu.HBM)
PROB, RATE, DUAL_RATE, DAMP, FLAG, SECTION, PRODUCTS, TABLE = 0, 1, 2, 3, 5, 7, 9, 17


def shifted(block, axis, distance):
    devices = range(lax.axis_size(axis))
    route = [(i - distance, i) for i in devices if i - distance in devices]
    return lax.ppermute(block, axis, route)


def call(body, specs, outs, scratch=(), limit=4, places=None, work=0):
    return pl.pallas_call(
        body,
        out_shape=[jax.ShapeDtypeStruct(shape, dtype) for shape, dtype in outs],
        in_specs=specs,
        out_specs=places or [VM] * len(outs),
        scratch_shapes=list(scratch),
        cost_estimate=pl.CostEstimate(
            flops=work, bytes_accessed=work // 256, transcendentals=0
        ) if work else None,
        compiler_params=pltpu.CompilerParams(vmem_limit_bytes=limit * MIB),
    )


def lanes_of(ref, row, block):
    return ref[row : row + 1, block * TILE : (block + 1) * TILE]


def widened(column):
    return jnp.concatenate([column] * QUARTERS, axis=1)


def entry_of(table_ref, index):
    return widened(table_ref[index])


def group_sum(values, inside):
    row = lax.broadcasted_iota(jnp.int32, values.shape, 0)
    for step in (1, 2, 4):
        partner = jnp.where(
            (row & step) != 0,
            pltpu.roll(values, step, 0),
            pltpu.roll(values, ROWS - step, 0),
        )
        values = jnp.where(inside > step, values + partner, values)
    return values


def halves(values):
    high = values.astype(BF16)
    return high, (values - high.astype(F32)).astype(BF16)


def product_images(lhs_ref, high_ref, low_ref, image_ref, transposed, ready=None):
    rows = lhs_ref.shape[0]
    high, low = halves(lhs_ref[...])
    both = jnp.concatenate([high, low], axis=0)
    dims = (((1,), (0,)), ((), ())) if transposed else (((1,), (1,)), ((), ()))

    def dot(a, b):
        return lax.dot_general(a, b, dims, preferred_element_type=F32)

    for j in range(NPOOL):
        if ready is not None:
            ready(j)
        main = dot(both, high_ref[j])
        image_ref[j] = main[:rows] + main[rows:] + dot(high, low_ref[j])


def code_of(code_refs, period, block, k):
    return tuple(ref[k, period, block] for ref in code_refs)


def gathered_blocks(image_ref, code_refs, period, block, height, slot):
    total = None
    for k in range(NB):
        which, place = code_of(code_refs, period, block, k)
        first = pl.multiple_of((slot * RB + place) * height, height)
        part = image_ref[which, pl.ds(first, height), :]
        total = part if total is None else total + part
    return total


def scattered_blocks(image_ref, code_refs, out_ref, height, period):
    top = period * RB * height
    out_ref[top : top + RB * height, :] = jnp.zeros((RB * height, TILE), F32)
    for block in range(RB):
        first = top + block * height
        for k in range(NB):
            which, column = code_of(code_refs, period, block, k)
            part = image_ref[which, first : first + height, :]
            place = pl.multiple_of((period * RB + column) * height, height)
            out_ref[pl.ds(place, height), :] += part


def fetch(pairs, sems):
    copies = [
        pltpu.make_async_copy(source, place, sems.at[i]) for i, (source, place) in enumerate(pairs)
    ]
    for copy in copies:
        copy.start()
    return copies


def carried_kernel(dual_hbm, demand_hbm, carry_hbm, prob_hbm, section_hbm, steps_hbm, subtree_hbm,
                   restart_hbm, carried_ref, late_ref, table_ref,
                   dual_ref, demand_ref, carry_ref, prob_ref, section_ref, steps_ref, subtree_ref,
                   restart_ref, sems):
    copies = fetch(
        [(prob_hbm, prob_ref), (section_hbm, section_ref), (steps_hbm, steps_ref),
         (subtree_hbm, subtree_ref), (restart_hbm, restart_ref), (carry_hbm, carry_ref),
         (dual_hbm, dual_ref), (demand_hbm, demand_ref)], sems)
    for copy in copies[:6]:
        copy.wait()
    device = lax.axis_index("scen")
    share = lax.axis_size("scen") // SUBTREES
    shape = (ROWS, LANES)
    row = lax.broadcasted_iota(jnp.int32, shape, 0)
    column = jnp.zeros(shape, F32)
    for s in range(ROWS):
        column = jnp.where(row == s, prob_ref[s], column)
    entry = subtree_ref[device // share]
    rate, dual_rate = steps_ref[0, entry], steps_ref[1, entry]
    table_ref[PROB] = column
    table_ref[RATE] = jnp.full(shape, rate)
    table_ref[DUAL_RATE] = jnp.full(shape, dual_rate)
    damps = []
    for period in range(PER):
        damps.append(jnp.where(restart_ref[0, period] == 1, 0.5, 1.0).astype(F32))
        table_ref[DAMP + period] = jnp.full(shape, damps[period])
        table_ref[FLAG + period] = jnp.full(shape, restart_ref[1, period].astype(F32))
        table_ref[SECTION + period] = jnp.full(shape, section_ref[period].astype(F32))
    assert share == ROWS
    for subtree in range(SUBTREES):
        other = subtree_ref[subtree]
        value = steps_ref[0, other] * steps_ref[1, other]
        table_ref[PRODUCTS + subtree] = jnp.full(shape, value)
    late_ref[...] = table_ref[SECTION + 1]
    for copy in copies[6:]:
        copy.wait()
    factor = damps[0] * dual_rate
    for block in range(RB):
        lanes = slice(block * TILE, (block + 1) * TILE)
        weight = lanes_of(carry_ref, 0, block)
        a = dual_ref[:, 0, lanes]
        carried_ref[block, 0:ROWS, :] = weight * a
        carried_ref[block, ROWS : 2 * ROWS, :] = weight * (a + factor * demand_ref[:, 0, lanes])


def pull_kernel(dual_hbm, demand_hbm, pool_hbm, carry_hbm, cost_hbm, cols_hbm, which_hbm, table_ref,
                raw_hbm, high_hbm, low_hbm, raw_ref, dual_ref, demand_ref, pool_ref, carry_ref, cost_ref,
                cols_ref, which_ref, high_ref, low_ref, lhs_ref, image_ref, sems, out_sems):
    copies = fetch(
        [(dual_hbm, dual_ref), (demand_hbm, demand_ref)]
        + [(pool_hbm.at[j], pool_ref.at[j]) for j in range(NPOOL)]
        + [(carry_hbm, carry_ref), (cost_hbm, cost_ref), (cols_hbm, cols_ref),
           (which_hbm, which_ref)], sems)
    written = []
    copies[0].wait()
    copies[1].wait()
    for period in range(PER):
        factor = entry_of(table_ref, DAMP + period) * entry_of(table_ref, DUAL_RATE)
        for block in range(RB):
            lanes = slice(block * TILE, (block + 1) * TILE)
            first = (period * RB + block) * 2 * ROWS
            a = dual_ref[:, period, lanes]
            lhs_ref[first : first + ROWS, :] = a
            lhs_ref[first + ROWS : first + 2 * ROWS, :] = a + factor * demand_ref[:, period, lanes]

    def ready(j):
        copies[2 + j].wait()
        high, low = halves(pool_ref[j])
        high_ref[j] = high
        low_ref[j] = low
        for i, (source, out) in enumerate(((high_ref, high_hbm), (low_ref, low_hbm))):
            copy = pltpu.make_async_copy(source.at[j], out.at[j], out_sems.at[2 * j + i])
            copy.start()
            written.append(copy)

    product_images(lhs_ref, high_ref, low_ref, image_ref, True, ready)
    for copy in copies[5:]:
        copy.wait()
    rate = jnp.concatenate([entry_of(table_ref, RATE)] * 2, axis=0)
    for period in range(PER):
        scattered_blocks(image_ref, (which_ref, cols_ref), raw_ref, 2 * ROWS, period)
        for block in range(RB):
            first = (period * RB + block) * 2 * ROWS
            here = slice(first, first + 2 * ROWS)
            value = raw_ref[here, :] - lanes_of(cost_ref, period, block)
            if period == 0:
                later = (RB + block) * 2 * ROWS
                value -= lanes_of(carry_ref, 1, block) * lhs_ref[later : later + 2 * ROWS, :]
            raw_ref[here, :] = rate * value
        half = pl.ds(period * RB * 2 * ROWS, RB * 2 * ROWS)
        copy = pltpu.make_async_copy(raw_ref.at[half], raw_hbm.at[half], out_sems.at[6 + period])
        copy.start()
        written.append(copy)
    for copy in written:
        copy.wait()


def local_kernel(raw_ref, arriving_ref, upper_ref, table_ref, before_ref,
                 kept_ref, message_ref, chunk_ref):
    place = pl.multiple_of(lax.axis_index("scen") * LANES, LANES)
    chunk_ref[PER] = before_ref[...]
    rate = entry_of(table_ref, RATE)
    product = rate * entry_of(table_ref, DUAL_RATE)
    weight = entry_of(table_ref, PROB)
    mass = jnp.sum(weight, axis=0, keepdims=True)
    for period in range(PER):
        section = entry_of(table_ref, SECTION + period)
        inverse = 1.0 / group_sum(weight, section)
        wide = section[0:1] > ROWS
        for block in range(RB):
            first = (period * RB + block) * 2 * ROWS
            raw = raw_ref[first : first + ROWS, :]
            other = raw_ref[first + ROWS : first + 2 * ROWS, :]
            if period == 1:
                raw -= rate * arriving_ref[block, 0:ROWS, :]
                other -= rate * arriving_ref[block, ROWS : 2 * ROWS, :]
            averaged = group_sum(weight * raw, section) * inverse
            second = group_sum(weight * other, section) * inverse
            new = jnp.minimum(jnp.maximum(averaged, 0.0), lanes_of(upper_ref, period, block))
            kept_ref[0, period, block] = new
            kept_ref[1, period, block] = second
            pushed = jnp.sum(product * weight * new, axis=0, keepdims=True)
            sums = jnp.where(wide, mass * averaged[0:1], pushed)
            second_sums = mass * second[0:1]
            for quarter in range(QUARTERS):
                lanes = slice(quarter * LANES, (quarter + 1) * LANES)
                chunk = block * QUARTERS + quarter
                message_ref[chunk, :, part_of(period)] = sums[:, lanes]
                message_ref[chunk, :, part_of(2 + period)] = second_sums[:, lanes]
        chunk_ref[period] = jnp.broadcast_to(
            upper_ref[period : period + 1, pl.ds(place, LANES)], (ROWS, LANES)
        )
    for chunk in range(RB * QUARTERS):
        message_ref[chunk, :, part_of(4)] = mass[:, :LANES]


def part_of(index):
    return slice(index * LANES, (index + 1) * LANES)


def reduce_kernel(got_ref, chunk_ref, table_ref, back_ref, mean_ref, moment_ref):
    devices = got_ref.shape[0]
    row = lax.broadcasted_iota(jnp.int32, (devices, devices), 0)
    column = lax.broadcasted_iota(jnp.int32, (devices, devices), 1)

    def member(section):
        span = jnp.maximum(section[0:1, 0:devices].astype(jnp.int32) // ROWS, 1)
        return ((row & -span) == (column & -span)).astype(F32)

    def dot(a, b):
        return jnp.dot(a, b, precision=lax.Precision.HIGHEST, preferred_element_type=F32)

    device = lax.axis_index("scen")
    mass = got_ref[:, 0, part_of(4)]
    moment = mass * table_ref[PRODUCTS:TABLE].reshape(devices, LANES)
    befores = (chunk_ref[PER], table_ref[SECTION])
    for period in range(PER):
        section = table_ref[SECTION + period]
        same = member(section)
        inverse = 1.0 / dot(same, mass)
        sums = got_ref[:, 0, part_of(period)]
        upper = chunk_ref[period, 0:1, :]
        new = jnp.minimum(jnp.maximum(dot(same, sums) * inverse, 0.0), upper)
        back_ref[:, 0, part_of(period)] = new
        back_ref[:, 0, part_of(2 + period)] = dot(same, got_ref[:, 0, part_of(2 + period)]) * inverse
        moment_ref[...] = dot(same, moment) * inverse
        mean_ref[period] = jnp.broadcast_to(moment_ref[pl.ds(device, 1), :], (ROWS, LANES))
        source = jnp.where(section[0:1] > ROWS, moment * new, sums)
        same = member(befores[period])
        back_ref[:, 0, part_of(4 + period)] = dot(same, source) / dot(same, mass)


def row_of(returned_ref, index, block):
    parts = [
        returned_ref[block * QUARTERS + quarter, :, part_of(index)] for quarter in range(QUARTERS)
    ]
    return jnp.concatenate(parts, axis=1)


def select_kernel(returned_ref, kept_ref, table_ref, chunk_ref,
                  early_ref, late_ref, second_ref, pushed_first_ref, pushed_next_ref):
    product = entry_of(table_ref, RATE) * entry_of(table_ref, DUAL_RATE)
    weight = entry_of(table_ref, PROB)
    befores = (entry_of(chunk_ref, PER), entry_of(table_ref, SECTION))
    for period in range(PER):
        out_ref = (early_ref, late_ref)[period]
        pushed_ref = (pushed_first_ref, pushed_next_ref)[period]
        wide = entry_of(table_ref, SECTION + period) > ROWS
        wide_before = befores[period] > ROWS
        scale = product / group_sum(weight, befores[period])
        for block in range(RB):
            shape = (ROWS, TILE)
            row = jnp.broadcast_to(row_of(returned_ref, period, block), shape)
            new = jnp.where(wide, row, kept_ref[0, period, block])
            out_ref[block] = new
            row = jnp.broadcast_to(row_of(returned_ref, 2 + period, block), shape)
            second_ref[period, block] = jnp.where(wide, row, kept_ref[1, period, block])
            row = jnp.broadcast_to(row_of(returned_ref, 4 + period, block), shape)
            averaged = scale * group_sum(weight * new, befores[period])
            pushed_ref[block] = jnp.where(wide_before, row, averaged)


def push_first_kernel(pushed_ref, high_ref, low_ref, carry_ref, table_ref, cols_hbm, which_hbm,
                      first_ref, lhs_ref, image_ref, cols_ref, which_ref, sems):
    copies = fetch([(cols_hbm, cols_ref), (which_hbm, which_ref)], sems)
    code_refs = which_ref, cols_ref
    for block in range(RB):
        lhs_ref[block * ROWS : (block + 1) * ROWS, :] = pushed_ref[block]
    product_images(lhs_ref, high_ref, low_ref, image_ref, False)
    for copy in copies:
        copy.wait()
    factor = 2.0 * entry_of(table_ref, DAMP)
    for block in range(RB):
        carry = lanes_of(carry_ref, 0, block)
        image = gathered_blocks(image_ref, code_refs, 0, block, ROWS, 0)
        first_ref[block] = factor * carry * image
        row = block % ROWS
        first_ref[RB + block // ROWS, row : row + 1, :] = 0.5 * factor[0:1] * carry * carry


def push_kernel(early_ref, late_ref, pushed_ref, high_ref, low_ref, carry_ref, table_ref,
                cols_hbm, which_hbm, image_out_ref, next_ref, lhs_ref, image_ref,
                cols_ref, which_ref, sems):
    copies = fetch([(cols_hbm, cols_ref), (which_hbm, which_ref)], sems)
    code_refs = which_ref, cols_ref
    for slot, field_ref in enumerate((early_ref, late_ref, pushed_ref)):
        for block in range(RB):
            first = (slot * RB + block) * ROWS
            lhs_ref[first : first + ROWS, :] = field_ref[block]
    product_images(lhs_ref, high_ref, low_ref, image_ref, False)
    for copy in copies:
        copy.wait()
    factor = 2.0 * entry_of(table_ref, DAMP + 1)
    for block in range(RB):
        for period in range(PER):
            image_out_ref[period, block] = gathered_blocks(
                image_ref, code_refs, period, block, ROWS, period
            )
        image = gathered_blocks(image_ref, code_refs, 1, block, ROWS, 2)
        next_ref[block] = factor * lanes_of(carry_ref, 1, block) * image


def net_kernel(early_ref, before_ref, images_ref, mean_ref, carry_ref, high_ref, low_ref, table_ref,
               cols_hbm, which_hbm, net_ref, pulled_ref, lhs_ref, image_ref,
               cols_ref, which_ref, sems):
    copies = fetch([(cols_hbm, cols_ref), (which_hbm, which_ref)], sems)
    code_refs = which_ref, cols_ref
    for period in range(PER):
        previous_ref = (before_ref, early_ref)[period]
        factor = entry_of(table_ref, DAMP + period) * widened(mean_ref[period])
        for block in range(RB):
            carry = lanes_of(carry_ref, period, block)
            net = 2.0 * (images_ref[period, block] - carry * previous_ref[block])
            net_ref[period, block] = net
            first = (period * RB + block) * ROWS
            lhs_ref[first : first + ROWS, :] = factor * net
    product_images(lhs_ref, high_ref, low_ref, image_ref, True)
    for copy in copies:
        copy.wait()
    for period in range(PER):
        scattered_blocks(image_ref, code_refs, pulled_ref, ROWS, period)


def primal_kernel(early_ref, late_ref, pulled_ref, second_ref, near_ref, far_ref, mean_ref,
                  upper_ref, carry_ref, table_ref, primal_ref, early_probe_ref, late_probe_ref):
    for period in range(PER):
        new_ref = (early_ref, late_ref)[period]
        next_ref = (near_ref, far_ref)[period]
        probe_ref = (early_probe_ref, late_probe_ref)[period]
        damp = entry_of(table_ref, DAMP + period)
        mean = 2.0 * widened(mean_ref[period])
        if period == 0:
            mean *= entry_of(table_ref, DAMP + 1)
        for block in range(RB):
            if period == 0:
                carry = lanes_of(carry_ref, 1, block)
                square = carry * carry
            else:
                row = block % ROWS
                square = far_ref[RB + block // ROWS, row : row + 1, :]
            first = (period * RB + block) * ROWS
            new = new_ref[block]
            primal = damp * new
            averaged = (
                primal + second_ref[period, block] - pulled_ref[first : first + ROWS, :]
                + next_ref[block] - square * mean * new
            )
            primal_new = jnp.minimum(jnp.maximum(averaged, 0.0), lanes_of(upper_ref, period, block))
            primal_ref[period, block] = primal_new
            probe_ref[block] = 2.0 * primal_new - primal


def result_kernel(early_probe_ref, late_probe_ref, high_ref, low_ref, dual_ref, demand_ref, net_ref,
                  early_ref, late_ref, new_ref, carry_ref, table_ref, cols_hbm, which_hbm,
                  primal_hbm, out_ref, primal_ref, lhs_ref, image_ref,
                  cols_ref, which_ref, sems, out_sem):
    copies = fetch([(cols_hbm, cols_ref), (which_hbm, which_ref)], sems)
    code_refs = which_ref, cols_ref
    for period in range(PER):
        probe_ref = (early_probe_ref, late_probe_ref)[period]
        first_ref = (early_ref, late_ref)[period]
        count = 2.0 * entry_of(table_ref, DAMP + period)
        flagged = entry_of(table_ref, FLAG + period) == 1.0
        share = 1.0 / (count + 1.0)
        for block in range(RB):
            first = (period * RB + block) * ROWS
            lhs_ref[first : first + ROWS, :] = probe_ref[block]
            primal_new = new_ref[period, block]
            primal_mean = (count * (0.5 * first_ref[block]) + primal_new) * share
            lanes = slice(block * TILE, (block + 1) * TILE)
            primal_ref[:, period, lanes] = jnp.where(flagged, primal_mean, primal_new)
    written = pltpu.make_async_copy(primal_ref, primal_hbm, out_sem.at[0])
    written.start()
    product_images(lhs_ref, high_ref, low_ref, image_ref, False)
    for copy in copies:
        copy.wait()
    dual_rate = entry_of(table_ref, DUAL_RATE)
    for period in range(PER):
        damp = entry_of(table_ref, DAMP + period)
        count = 2.0 * damp
        flagged = entry_of(table_ref, FLAG + period) == 1.0
        share = 1.0 / (count + 1.0)
        for block in range(RB):
            lanes = slice(block * TILE, (block + 1) * TILE)
            start, target = dual_ref[:, period, lanes], demand_ref[:, period, lanes]
            change = dual_rate * (target - net_ref[period, block])
            image = gathered_blocks(image_ref, code_refs, period, block, ROWS, period)
            if period == 1:
                image -= lanes_of(carry_ref, 1, block) * early_probe_ref[block]
            dual_new = start + damp * change + dual_rate * (target - image)
            dual_mean = (count * (start + 0.5 * change) + dual_new) * share
            out_ref[:, period, lanes] = jnp.where(flagged, dual_mean, dual_new)
    written.wait()


def correct_kernel(partial_ref, before_ref, carry_ref, table_ref, out_hbm, out_ref, added_ref, sems):
    share = 1.0 / (2.0 * entry_of(table_ref, DAMP) + 1.0)
    factor = entry_of(table_ref, DUAL_RATE) * jnp.where(
        entry_of(table_ref, FLAG) == 1.0, share, 1.0
    )
    for block in range(RB):
        added_ref[:, block * TILE : (block + 1) * TILE] = (
            factor * lanes_of(carry_ref, 0, block) * before_ref[block]
        )
    copies = []
    for s in range(ROWS):
        out_ref[s, 0:1, :] = partial_ref[s, 0:1, :] + added_ref[s : s + 1, :]
        out_ref[s, 1:2, :] = partial_ref[s, 1:2, :]
        copy = pltpu.make_async_copy(out_ref.at[s], out_hbm.at[s], sems.at[s])
        copy.start()
        copies.append(copy)
    for copy in copies:
        copy.wait()


def per_device(
    dual_start,
    demand,
    cost,
    upper,
    carry,
    prob,
    section_size,
    block_cols,
    block_pool,
    pool_tiles,
    step_table,
    subtree_step,
    restart,
):
    rows, periods, feature = dual_start.shape
    devices = lax.axis_size("scen")
    field = (PER, RB, ROWS, TILE)
    slab = (RB, ROWS, TILE)
    tiles = (NPOOL, TILE, TILE)
    packed = (PER, feature)

    def scratch(height, slots=PER):
        count = slots * RB * height
        return [pltpu.VMEM((count, TILE), F32), pltpu.VMEM((NPOOL, count, TILE), F32)]

    codes = (block_cols.transpose(2, 0, 1), block_pool.transpose(2, 0, 1))
    code_scratch = [
        pltpu.SMEM((NB, PER, RB), jnp.int32), pltpu.SMEM((NB, PER, RB), jnp.int32),
        pltpu.SemaphoreType.DMA((2,)),
    ]
    heavy = 2 * 3 * NPOOL * TILE * TILE * PER * RB * ROWS

    with jax.named_scope("carried"):
        carried, late_section, table = call(
            carried_kernel, [FAR] * 8,
            [((RB, 2 * ROWS, TILE), F32), ((ROWS, LANES), F32), ((TABLE, ROWS, LANES), F32)],
            [pltpu.VMEM(dual_start.shape, F32), pltpu.VMEM(dual_start.shape, F32),
             pltpu.VMEM(packed, F32), pltpu.SMEM((ROWS,), F32), pltpu.SMEM((PER,), jnp.int32),
             pltpu.SMEM(step_table.shape[::-1], F32), pltpu.SMEM((SUBTREES,), jnp.int32),
             pltpu.SMEM(restart.shape, jnp.int32),
             pltpu.SemaphoreType.DMA((8,))], 60,
        )(dual_start, demand, carry, prob, section_size, step_table.T, subtree_step, restart)
    arriving = shifted(carried, "per", -1)
    before = shifted(late_section, "per", 1)
    with jax.named_scope("first_pull"):
        raw, high, low = call(
            pull_kernel, [FAR] * 7 + [VM],
            [((PER * RB * 2 * ROWS, TILE), F32), (tiles, BF16), (tiles, BF16)],
            [pltpu.VMEM((PER * RB * 2 * ROWS, TILE), F32),
             pltpu.VMEM(dual_start.shape, F32), pltpu.VMEM(dual_start.shape, F32),
             pltpu.VMEM(tiles, F32), pltpu.VMEM(packed, F32), pltpu.VMEM(packed, F32),
             pltpu.SMEM((NB, PER, RB), jnp.int32), pltpu.SMEM((NB, PER, RB), jnp.int32),
             pltpu.VMEM(tiles, BF16), pltpu.VMEM(tiles, BF16)]
            + scratch(2 * ROWS) + [pltpu.SemaphoreType.DMA((9,)), pltpu.SemaphoreType.DMA((8,))],
            60, [FAR, FAR, FAR], 2 * heavy,
        )(dual_start, demand, pool_tiles, carry, cost, *codes, table)
    with jax.named_scope("local_average"):
        kept, message, chunk = call(
            local_kernel, [VM] * 5,
            [((2,) + field, F32), ((devices, 1, 5 * LANES), F32), ((PER + 1, ROWS, LANES), F32)],
        )(raw, arriving, upper, table, before)
    got = lax.all_to_all(message, "scen", 0, 0, tiled=True)
    with jax.named_scope("section_average"):
        back, mean = call(
            reduce_kernel, [VM] * 3, [((devices, 1, 6 * LANES), F32), ((PER, ROWS, LANES), F32)],
            [pltpu.VMEM((devices, LANES), F32)],
        )(got, chunk, table)
    returned = lax.all_to_all(back, "scen", 0, 0, tiled=True)
    with jax.named_scope("selected"):
        early, late, second, pushed_first, pushed_next = call(
            select_kernel, [VM] * 4,
            [(slab, F32), (slab, F32), (field, F32), (slab, F32), (slab, F32)],
        )(returned, kept, table, chunk)
    new_before = shifted(late, "per", 1)
    with jax.named_scope("push_first"):
        (first,) = call(
            push_first_kernel, [VM] * 5 + [FAR] * 2, [((RB + RB // ROWS, ROWS, TILE), F32)],
            scratch(ROWS, 1) + code_scratch, 6, work=heavy // 2,
        )(pushed_first, high, low, carry, table, *codes)
    far = shifted(first, "per", -1)
    early, late, pushed_next, first = lax.optimization_barrier((early, late, pushed_next, first))
    with jax.named_scope("push"):
        images, near = call(
            push_kernel, [VM] * 7 + [FAR] * 2, [(field, F32), (slab, F32)],
            scratch(ROWS, 3) + code_scratch, 10, work=2 * heavy,
        )(early, late, pushed_next, high, low, carry, table, *codes)
    with jax.named_scope("second_pull"):
        net, pulled = call(
            net_kernel, [VM] * 8 + [FAR] * 2, [(field, F32), ((PER * RB * ROWS, TILE), F32)],
            scratch(ROWS) + code_scratch, 8, work=heavy,
        )(early, new_before, images, mean, carry, high, low, table, *codes)
    far, pulled = lax.optimization_barrier((far, pulled))
    with jax.named_scope("second_primal"):
        primal_new, early_probe, late_probe = call(
            primal_kernel, [VM] * 10, [(field, F32), (slab, F32), (slab, F32)],
        )(early, late, pulled, second, near, far, mean, upper, carry, table)
    probe_before = shifted(late_probe, "per", 1)
    with jax.named_scope("second_push"):
        primal, partial = call(
            result_kernel, [VM] * 12 + [FAR] * 2, [(dual_start.shape, F32), (dual_start.shape, F32)],
            [pltpu.VMEM(dual_start.shape, F32)] + scratch(ROWS) + code_scratch
            + [pltpu.SemaphoreType.DMA((1,))], 8, [FAR, VM], heavy,
        )(early_probe, late_probe, high, low, dual_start, demand, net, early, late, primal_new,
          carry, table, *codes)
    with jax.named_scope("correction"):
        (dual,) = call(
            correct_kernel, [VM] * 4, [(dual_start.shape, F32)],
            [pltpu.VMEM(dual_start.shape, F32), pltpu.VMEM((ROWS, feature), F32),
             pltpu.SemaphoreType.DMA((ROWS,))], places=[FAR],
        )(partial, probe_before, carry, table)
    return primal, dual


def solution(mesh):
    return jax.shard_map(
        per_device,
        mesh=mesh,
        in_specs=(
            P("scen", "per", None),
            P("scen", "per", None),
            P("per", None),
            P("per", None),
            P("per", None),
            P("scen"),
            P("per"),
            P("per", None, None),
            P("per", None, None),
            P(),
            P(),
            P(),
            P(None, "per"),
        ),
        out_specs=(P("scen", "per", None), P("scen", "per", None)),
        check_vma=False,
    )
```

```python
import functools

import jax
import jax.numpy as jnp
from jax import lax
from jax.experimental import pallas as pl
from jax.experimental.pallas import tpu as pltpu
from jax.sharding import PartitionSpec as P

TILE = 512
NPOOL = 3
NB = 3
SUBTREES = 8
RB = 16
LANES = 128
ROWS = 8
PER = 2
QUARTERS = TILE // LANES
MIB = 1 << 20
F32 = jnp.float32
BF16 = jnp.bfloat16

VM = pl.BlockSpec(memory_space=pltpu.VMEM)
SM = pl.BlockSpec(memory_space=pltpu.SMEM)
FAR = pl.BlockSpec(memory_space=pltpu.HBM)
PROB, RATE, DUAL_RATE, DAMP, FLAG, SECTION, PRODUCTS, TABLE = 0, 1, 2, 3, 5, 7, 9, 17


def shifted(block, axis, distance):
    devices = range(lax.axis_size(axis))
    route = [(i - distance, i) for i in devices if i - distance in devices]
    return lax.ppermute(block, axis, route)


def call(body, specs, outs, scratch=(), limit=4, places=None, work=0):
    return pl.pallas_call(
        body,
        out_shape=[jax.ShapeDtypeStruct(shape, dtype) for shape, dtype in outs],
        in_specs=specs,
        out_specs=places or [VM] * len(outs),
        scratch_shapes=list(scratch),
        cost_estimate=pl.CostEstimate(
            flops=work, bytes_accessed=work // 256, transcendentals=0
        ) if work else None,
        compiler_params=pltpu.CompilerParams(vmem_limit_bytes=limit * MIB),
    )


def lanes_of(ref, row, block):
    return ref[row : row + 1, block * TILE : (block + 1) * TILE]


def widened(column):
    return jnp.concatenate([column] * QUARTERS, axis=1)


def entry_of(table_ref, index):
    return widened(table_ref[index])


def group_sum(values, inside):
    row = lax.broadcasted_iota(jnp.int32, values.shape, 0)
    for step in (1, 2, 4):
        partner = jnp.where(
            (row & step) != 0,
            pltpu.roll(values, step, 0),
            pltpu.roll(values, ROWS - step, 0),
        )
        values = jnp.where(inside > step, values + partner, values)
    return values


def halves(values):
    high = values.astype(BF16)
    return high, (values - high.astype(F32)).astype(BF16)


def product_images(lhs_ref, high_ref, low_ref, image_ref, transposed, ready=None):
    rows = lhs_ref.shape[0]
    high, low = halves(lhs_ref[...])
    both = jnp.concatenate([high, low], axis=0)
    dims = (((1,), (0,)), ((), ())) if transposed else (((1,), (1,)), ((), ()))

    def dot(a, b):
        return lax.dot_general(a, b, dims, preferred_element_type=F32)

    for j in range(NPOOL):
        if ready is not None:
            ready(j)
        main = dot(both, high_ref[j])
        image_ref[j] = main[:rows] + main[rows:] + dot(high, low_ref[j])


def code_of(code_refs, period, block, k):
    return tuple(ref[k, period, block] for ref in code_refs)


def gathered_blocks(image_ref, code_refs, period, block, height, slot):
    total = None
    for k in range(NB):
        which, place = code_of(code_refs, period, block, k)
        first = pl.multiple_of((slot * RB + place) * height, height)
        part = image_ref[which, pl.ds(first, height), :]
        total = part if total is None else total + part
    return total


def scattered_blocks(image_ref, code_refs, out_ref, height, period, slot):
    top = slot * RB * height
    out_ref[top : top + RB * height, :] = jnp.zeros((RB * height, TILE), F32)
    for block in range(RB):
        first = top + block * height
        for k in range(NB):
            which, column = code_of(code_refs, period, block, k)
            part = image_ref[which, first : first + height, :]
            place = pl.multiple_of((slot * RB + column) * height, height)
            out_ref[pl.ds(place, height), :] += part


def fetch(pairs, sems):
    copies = [
        pltpu.make_async_copy(source, place, sems.at[i]) for i, (source, place) in enumerate(pairs)
    ]
    for copy in copies:
        copy.start()
    return copies


def carried_kernel(dual_hbm, demand_hbm, carry_hbm, prob_hbm, section_hbm, steps_hbm, subtree_hbm,
                   restart_hbm, carried_ref, late_ref, table_ref,
                   dual_ref, demand_ref, carry_ref, prob_ref, section_ref, steps_ref, subtree_ref,
                   restart_ref, sems):
    copies = fetch(
        [(prob_hbm, prob_ref), (section_hbm, section_ref), (steps_hbm, steps_ref),
         (subtree_hbm, subtree_ref), (restart_hbm, restart_ref), (carry_hbm, carry_ref),
         (dual_hbm, dual_ref), (demand_hbm, demand_ref)], sems)
    for copy in copies[:6]:
        copy.wait()
    device = lax.axis_index("scen")
    share = lax.axis_size("scen") // SUBTREES
    shape = (ROWS, LANES)
    row = lax.broadcasted_iota(jnp.int32, shape, 0)
    column = jnp.zeros(shape, F32)
    for s in range(ROWS):
        column = jnp.where(row == s, prob_ref[s], column)
    entry = subtree_ref[device // share]
    rate, dual_rate = steps_ref[0, entry], steps_ref[1, entry]
    table_ref[PROB] = column
    table_ref[RATE] = jnp.full(shape, rate)
    table_ref[DUAL_RATE] = jnp.full(shape, dual_rate)
    damps = []
    for period in range(PER):
        damps.append(jnp.where(restart_ref[0, period] == 1, 0.5, 1.0).astype(F32))
        table_ref[DAMP + period] = jnp.full(shape, damps[period])
        table_ref[FLAG + period] = jnp.full(shape, restart_ref[1, period].astype(F32))
        table_ref[SECTION + period] = jnp.full(shape, section_ref[period].astype(F32))
    assert share == ROWS
    for subtree in range(SUBTREES):
        other = subtree_ref[subtree]
        value = steps_ref[0, other] * steps_ref[1, other]
        table_ref[PRODUCTS + subtree] = jnp.full(shape, value)
    late_ref[...] = table_ref[SECTION + 1]
    for copy in copies[6:]:
        copy.wait()
    factor = damps[0] * dual_rate
    for block in range(RB):
        lanes = slice(block * TILE, (block + 1) * TILE)
        weight = lanes_of(carry_ref, 0, block)
        a = dual_ref[:, 0, lanes]
        carried_ref[block, 0:ROWS, :] = weight * a
        carried_ref[block, ROWS : 2 * ROWS, :] = weight * (a + factor * demand_ref[:, 0, lanes])


def pull_kernel(dual_hbm, demand_hbm, pool_hbm, carry_hbm, cost_hbm, cols_hbm, which_hbm, table_ref,
                raw_hbm, high_hbm, low_hbm, raw_ref, dual_ref, demand_ref, pool_ref, carry_ref, cost_ref,
                cols_ref, which_ref, high_ref, low_ref, lhs_ref, image_ref, sems, out_sems):
    copies = fetch(
        [(dual_hbm, dual_ref), (demand_hbm, demand_ref)]
        + [(pool_hbm.at[j], pool_ref.at[j]) for j in range(NPOOL)]
        + [(carry_hbm, carry_ref), (cost_hbm, cost_ref), (cols_hbm, cols_ref),
           (which_hbm, which_ref)], sems)
    written = []
    copies[0].wait()
    copies[1].wait()
    for period in range(PER):
        factor = entry_of(table_ref, DAMP + period) * entry_of(table_ref, DUAL_RATE)
        for block in range(RB):
            lanes = slice(block * TILE, (block + 1) * TILE)
            first = (period * RB + block) * 2 * ROWS
            a = dual_ref[:, period, lanes]
            lhs_ref[first : first + ROWS, :] = a
            lhs_ref[first + ROWS : first + 2 * ROWS, :] = a + factor * demand_ref[:, period, lanes]

    def ready(j):
        copies[2 + j].wait()
        high, low = halves(pool_ref[j])
        high_ref[j] = high
        low_ref[j] = low
        for i, (source, out) in enumerate(((high_ref, high_hbm), (low_ref, low_hbm))):
            copy = pltpu.make_async_copy(source.at[j], out.at[j], out_sems.at[2 * j + i])
            copy.start()
            written.append(copy)

    product_images(lhs_ref, high_ref, low_ref, image_ref, True, ready)
    for copy in copies[5:]:
        copy.wait()
    rate = jnp.concatenate([entry_of(table_ref, RATE)] * 2, axis=0)
    for period in range(PER):
        scattered_blocks(image_ref, (which_ref, cols_ref), raw_ref, 2 * ROWS, period, period)
        for block in range(RB):
            first = (period * RB + block) * 2 * ROWS
            here = slice(first, first + 2 * ROWS)
            value = raw_ref[here, :] - lanes_of(cost_ref, period, block)
            if period == 0:
                later = (RB + block) * 2 * ROWS
                value -= lanes_of(carry_ref, 1, block) * lhs_ref[later : later + 2 * ROWS, :]
            raw_ref[here, :] = rate * value
        half = pl.ds(period * RB * 2 * ROWS, RB * 2 * ROWS)
        copy = pltpu.make_async_copy(raw_ref.at[half], raw_hbm.at[half], out_sems.at[6 + period])
        copy.start()
        written.append(copy)
    for copy in written:
        copy.wait()


def local_kernel(raw_ref, arriving_ref, upper_ref, table_ref, before_ref,
                 kept_ref, message_ref, chunk_ref):
    place = pl.multiple_of(lax.axis_index("scen") * LANES, LANES)
    chunk_ref[PER] = before_ref[...]
    rate = entry_of(table_ref, RATE)
    product = rate * entry_of(table_ref, DUAL_RATE)
    weight = entry_of(table_ref, PROB)
    mass = jnp.sum(weight, axis=0, keepdims=True)
    for period in range(PER):
        section = entry_of(table_ref, SECTION + period)
        inverse = 1.0 / group_sum(weight, section)
        wide = section[0:1] > ROWS
        for block in range(RB):
            first = (period * RB + block) * 2 * ROWS
            raw = raw_ref[first : first + ROWS, :]
            other = raw_ref[first + ROWS : first + 2 * ROWS, :]
            if period == 1:
                raw -= rate * arriving_ref[block, 0:ROWS, :]
                other -= rate * arriving_ref[block, ROWS : 2 * ROWS, :]
            averaged = group_sum(weight * raw, section) * inverse
            second = group_sum(weight * other, section) * inverse
            new = jnp.minimum(jnp.maximum(averaged, 0.0), lanes_of(upper_ref, period, block))
            kept_ref[0, period, block] = new
            kept_ref[1, period, block] = second
            pushed = jnp.sum(product * weight * new, axis=0, keepdims=True)
            sums = jnp.where(wide, mass * averaged[0:1], pushed)
            second_sums = mass * second[0:1]
            for quarter in range(QUARTERS):
                lanes = slice(quarter * LANES, (quarter + 1) * LANES)
                chunk = block * QUARTERS + quarter
                message_ref[chunk, :, part_of(period)] = sums[:, lanes]
                message_ref[chunk, :, part_of(2 + period)] = second_sums[:, lanes]
        chunk_ref[period] = jnp.broadcast_to(
            upper_ref[period : period + 1, pl.ds(place, LANES)], (ROWS, LANES)
        )
    for chunk in range(RB * QUARTERS):
        message_ref[chunk, :, part_of(4)] = mass[:, :LANES]


def part_of(index):
    return slice(index * LANES, (index + 1) * LANES)


def reduce_kernel(got_ref, chunk_ref, table_ref, back_ref, mean_ref, moment_ref):
    devices = got_ref.shape[0]
    row = lax.broadcasted_iota(jnp.int32, (devices, devices), 0)
    column = lax.broadcasted_iota(jnp.int32, (devices, devices), 1)

    def member(section):
        span = jnp.maximum(section[0:1, 0:devices].astype(jnp.int32) // ROWS, 1)
        return ((row & -span) == (column & -span)).astype(F32)

    def dot(a, b):
        return jnp.dot(a, b, precision=lax.Precision.HIGHEST, preferred_element_type=F32)

    device = lax.axis_index("scen")
    mass = got_ref[:, 0, part_of(4)]
    moment = mass * table_ref[PRODUCTS:TABLE].reshape(devices, LANES)
    befores = (chunk_ref[PER], table_ref[SECTION])
    for period in range(PER):
        section = table_ref[SECTION + period]
        same = member(section)
        inverse = 1.0 / dot(same, mass)
        sums = got_ref[:, 0, part_of(period)]
        upper = chunk_ref[period, 0:1, :]
        new = jnp.minimum(jnp.maximum(dot(same, sums) * inverse, 0.0), upper)
        back_ref[:, 0, part_of(period)] = new
        back_ref[:, 0, part_of(2 + period)] = dot(same, got_ref[:, 0, part_of(2 + period)]) * inverse
        moment_ref[...] = dot(same, moment) * inverse
        mean_ref[period] = jnp.broadcast_to(moment_ref[pl.ds(device, 1), :], (ROWS, LANES))
        source = jnp.where(section[0:1] > ROWS, moment * new, sums)
        same = member(befores[period])
        back_ref[:, 0, part_of(4 + period)] = dot(same, source) / dot(same, mass)


def row_of(returned_ref, index, block):
    parts = [
        returned_ref[block * QUARTERS + quarter, :, part_of(index)] for quarter in range(QUARTERS)
    ]
    return jnp.concatenate(parts, axis=1)


def select_kernel(returned_ref, kept_ref, table_ref, chunk_ref,
                  early_ref, late_ref, second_ref, pushed_first_ref, pushed_next_ref):
    product = entry_of(table_ref, RATE) * entry_of(table_ref, DUAL_RATE)
    weight = entry_of(table_ref, PROB)
    befores = (entry_of(chunk_ref, PER), entry_of(table_ref, SECTION))
    for period in range(PER):
        out_ref = (early_ref, late_ref)[period]
        pushed_ref = (pushed_first_ref, pushed_next_ref)[period]
        wide = entry_of(table_ref, SECTION + period) > ROWS
        wide_before = befores[period] > ROWS
        scale = product / group_sum(weight, befores[period])
        for block in range(RB):
            shape = (ROWS, TILE)
            row = jnp.broadcast_to(row_of(returned_ref, period, block), shape)
            new = jnp.where(wide, row, kept_ref[0, period, block])
            out_ref[block] = new
            row = jnp.broadcast_to(row_of(returned_ref, 2 + period, block), shape)
            second_ref[period, block] = jnp.where(wide, row, kept_ref[1, period, block])
            row = jnp.broadcast_to(row_of(returned_ref, 4 + period, block), shape)
            averaged = scale * group_sum(weight * new, befores[period])
            pushed_ref[block] = jnp.where(wide_before, row, averaged)


def push_first_kernel(pushed_ref, high_ref, low_ref, carry_ref, table_ref, cols_hbm, which_hbm,
                      first_ref, lhs_ref, image_ref, cols_ref, which_ref, sems):
    copies = fetch([(cols_hbm, cols_ref), (which_hbm, which_ref)], sems)
    code_refs = which_ref, cols_ref
    for block in range(RB):
        lhs_ref[block * ROWS : (block + 1) * ROWS, :] = pushed_ref[block]
    product_images(lhs_ref, high_ref, low_ref, image_ref, False)
    for copy in copies:
        copy.wait()
    factor = 2.0 * entry_of(table_ref, DAMP)
    for block in range(RB):
        carry = lanes_of(carry_ref, 0, block)
        image = gathered_blocks(image_ref, code_refs, 0, block, ROWS, 0)
        first_ref[block] = factor * carry * image
        row = block % ROWS
        first_ref[RB + block // ROWS, row : row + 1, :] = 0.5 * factor[0:1] * carry * carry


def push_late_kernel(late_ref, high_ref, low_ref, cols_hbm, which_hbm, out_ref, lhs_ref, image_ref,
                     cols_ref, which_ref, sems):
    copies = fetch([(cols_hbm, cols_ref), (which_hbm, which_ref)], sems)
    for block in range(RB):
        lhs_ref[block * ROWS : (block + 1) * ROWS, :] = late_ref[block]
    product_images(lhs_ref, high_ref, low_ref, image_ref, False)
    for copy in copies:
        copy.wait()
    for block in range(RB):
        out_ref[block] = gathered_blocks(image_ref, (which_ref, cols_ref), 1, block, ROWS, 0)


def push_early_kernel(early_ref, pushed_ref, high_ref, low_ref, carry_ref, table_ref,
                      cols_hbm, which_hbm, out_ref, next_ref, lhs_ref, image_ref,
                      cols_ref, which_ref, sems):
    copies = fetch([(cols_hbm, cols_ref), (which_hbm, which_ref)], sems)
    code_refs = which_ref, cols_ref
    for slot, slab_ref in enumerate((early_ref, pushed_ref)):
        for block in range(RB):
            first = (slot * RB + block) * ROWS
            lhs_ref[first : first + ROWS, :] = slab_ref[block]
    product_images(lhs_ref, high_ref, low_ref, image_ref, False)
    for copy in copies:
        copy.wait()
    factor = 2.0 * entry_of(table_ref, DAMP + 1)
    for block in range(RB):
        out_ref[block] = gathered_blocks(image_ref, code_refs, 0, block, ROWS, 0)
        image = gathered_blocks(image_ref, code_refs, 1, block, ROWS, 1)
        next_ref[block] = factor * lanes_of(carry_ref, 1, block) * image


def net_kernel(period, previous_ref, images_ref, mean_ref, carry_ref, high_ref, low_ref, table_ref,
               cols_hbm, which_hbm, net_ref, pulled_ref, lhs_ref, image_ref,
               cols_ref, which_ref, sems):
    copies = fetch([(cols_hbm, cols_ref), (which_hbm, which_ref)], sems)
    factor = entry_of(table_ref, DAMP + period) * widened(mean_ref[period])
    for block in range(RB):
        carry = lanes_of(carry_ref, period, block)
        net = 2.0 * (images_ref[block] - carry * previous_ref[block])
        net_ref[block] = net
        lhs_ref[block * ROWS : (block + 1) * ROWS, :] = factor * net
    product_images(lhs_ref, high_ref, low_ref, image_ref, True)
    for copy in copies:
        copy.wait()
    scattered_blocks(image_ref, (which_ref, cols_ref), pulled_ref, ROWS, period, 0)


def primal_kernel(period, new_ref, pulled_ref, second_ref, next_ref, mean_ref, upper_ref, carry_ref,
                  table_ref, primal_ref, probe_ref):
    damp = entry_of(table_ref, DAMP + period)
    mean = 2.0 * widened(mean_ref[period])
    if period == 0:
        mean *= entry_of(table_ref, DAMP + 1)
    for block in range(RB):
        if period == 0:
            carry = lanes_of(carry_ref, 1, block)
            square = carry * carry
        else:
            row = block % ROWS
            square = next_ref[RB + block // ROWS, row : row + 1, :]
        new = new_ref[block]
        primal = damp * new
        averaged = (
            primal + second_ref[period, block] - pulled_ref[block * ROWS : (block + 1) * ROWS, :]
            + next_ref[block] - square * mean * new
        )
        primal_new = jnp.minimum(jnp.maximum(averaged, 0.0), lanes_of(upper_ref, period, block))
        primal_ref[block] = primal_new
        probe_ref[block] = 2.0 * primal_new - primal


def result_kernel(early_probe_ref, late_probe_ref, high_ref, low_ref, dual_ref, demand_ref, early_net_ref,
                  late_net_ref, early_ref, late_ref, early_new_ref, late_new_ref, carry_ref, table_ref, cols_hbm, which_hbm,
                  primal_hbm, out_ref, primal_ref, lhs_ref, image_ref,
                  cols_ref, which_ref, sems, out_sem):
    copies = fetch([(cols_hbm, cols_ref), (which_hbm, which_ref)], sems)
    code_refs = which_ref, cols_ref
    for period in range(PER):
        probe_ref = (early_probe_ref, late_probe_ref)[period]
        first_ref = (early_ref, late_ref)[period]
        count = 2.0 * entry_of(table_ref, DAMP + period)
        flagged = entry_of(table_ref, FLAG + period) == 1.0
        share = 1.0 / (count + 1.0)
        for block in range(RB):
            first = (period * RB + block) * ROWS
            lhs_ref[first : first + ROWS, :] = probe_ref[block]
            primal_new = (early_new_ref, late_new_ref)[period][block]
            primal_mean = (count * (0.5 * first_ref[block]) + primal_new) * share
            lanes = slice(block * TILE, (block + 1) * TILE)
            primal_ref[:, period, lanes] = jnp.where(flagged, primal_mean, primal_new)
    written = pltpu.make_async_copy(primal_ref, primal_hbm, out_sem.at[0])
    written.start()
    product_images(lhs_ref, high_ref, low_ref, image_ref, False)
    for copy in copies:
        copy.wait()
    dual_rate = entry_of(table_ref, DUAL_RATE)
    for period in range(PER):
        damp = entry_of(table_ref, DAMP + period)
        count = 2.0 * damp
        flagged = entry_of(table_ref, FLAG + period) == 1.0
        share = 1.0 / (count + 1.0)
        for block in range(RB):
            lanes = slice(block * TILE, (block + 1) * TILE)
            start, target = dual_ref[:, period, lanes], demand_ref[:, period, lanes]
            change = dual_rate * (target - (early_net_ref, late_net_ref)[period][block])
            image = gathered_blocks(image_ref, code_refs, period, block, ROWS, period)
            if period == 1:
                image -= lanes_of(carry_ref, 1, block) * early_probe_ref[block]
            dual_new = start + damp * change + dual_rate * (target - image)
            dual_mean = (count * (start + 0.5 * change) + dual_new) * share
            out_ref[:, period, lanes] = jnp.where(flagged, dual_mean, dual_new)
    written.wait()


def correct_kernel(partial_ref, before_ref, carry_ref, table_ref, out_hbm, out_ref, added_ref, sems):
    share = 1.0 / (2.0 * entry_of(table_ref, DAMP) + 1.0)
    factor = entry_of(table_ref, DUAL_RATE) * jnp.where(
        entry_of(table_ref, FLAG) == 1.0, share, 1.0
    )
    for block in range(RB):
        added_ref[:, block * TILE : (block + 1) * TILE] = (
            factor * lanes_of(carry_ref, 0, block) * before_ref[block]
        )
    copies = []
    for s in range(ROWS):
        out_ref[s, 0:1, :] = partial_ref[s, 0:1, :] + added_ref[s : s + 1, :]
        out_ref[s, 1:2, :] = partial_ref[s, 1:2, :]
        copy = pltpu.make_async_copy(out_ref.at[s], out_hbm.at[s], sems.at[s])
        copy.start()
        copies.append(copy)
    for copy in copies:
        copy.wait()


def per_device(
    dual_start,
    demand,
    cost,
    upper,
    carry,
    prob,
    section_size,
    block_cols,
    block_pool,
    pool_tiles,
    step_table,
    subtree_step,
    restart,
):
    rows, periods, feature = dual_start.shape
    devices = lax.axis_size("scen")
    field = (PER, RB, ROWS, TILE)
    slab = (RB, ROWS, TILE)
    tiles = (NPOOL, TILE, TILE)
    packed = (PER, feature)

    def scratch(height, slots=PER):
        count = slots * RB * height
        return [pltpu.VMEM((count, TILE), F32), pltpu.VMEM((NPOOL, count, TILE), F32)]

    codes = (block_cols.transpose(2, 0, 1), block_pool.transpose(2, 0, 1))
    code_scratch = [
        pltpu.SMEM((NB, PER, RB), jnp.int32), pltpu.SMEM((NB, PER, RB), jnp.int32),
        pltpu.SemaphoreType.DMA((2,)),
    ]
    heavy = 2 * 3 * NPOOL * TILE * TILE * PER * RB * ROWS

    with jax.named_scope("carried"):
        carried, late_section, table = call(
            carried_kernel, [FAR] * 8,
            [((RB, 2 * ROWS, TILE), F32), ((ROWS, LANES), F32), ((TABLE, ROWS, LANES), F32)],
            [pltpu.VMEM(dual_start.shape, F32), pltpu.VMEM(dual_start.shape, F32),
             pltpu.VMEM(packed, F32), pltpu.SMEM((ROWS,), F32), pltpu.SMEM((PER,), jnp.int32),
             pltpu.SMEM(step_table.shape[::-1], F32), pltpu.SMEM((SUBTREES,), jnp.int32),
             pltpu.SMEM(restart.shape, jnp.int32),
             pltpu.SemaphoreType.DMA((8,))], 60,
        )(dual_start, demand, carry, prob, section_size, step_table.T, subtree_step, restart)
    arriving = shifted(carried, "per", -1)
    before = shifted(late_section, "per", 1)
    with jax.named_scope("first_pull"):
        raw, high, low = call(
            pull_kernel, [FAR] * 7 + [VM],
            [((PER * RB * 2 * ROWS, TILE), F32), (tiles, BF16), (tiles, BF16)],
            [pltpu.VMEM((PER * RB * 2 * ROWS, TILE), F32),
             pltpu.VMEM(dual_start.shape, F32), pltpu.VMEM(dual_start.shape, F32),
             pltpu.VMEM(tiles, F32), pltpu.VMEM(packed, F32), pltpu.VMEM(packed, F32),
             pltpu.SMEM((NB, PER, RB), jnp.int32), pltpu.SMEM((NB, PER, RB), jnp.int32),
             pltpu.VMEM(tiles, BF16), pltpu.VMEM(tiles, BF16)]
            + scratch(2 * ROWS) + [pltpu.SemaphoreType.DMA((9,)), pltpu.SemaphoreType.DMA((8,))],
            60, [FAR, FAR, FAR], 2 * heavy,
        )(dual_start, demand, pool_tiles, carry, cost, *codes, table)
    with jax.named_scope("local_average"):
        kept, message, chunk = call(
            local_kernel, [VM] * 5,
            [((2,) + field, F32), ((devices, 1, 5 * LANES), F32), ((PER + 1, ROWS, LANES), F32)],
        )(raw, arriving, upper, table, before)
    got = lax.all_to_all(message, "scen", 0, 0, tiled=True)
    with jax.named_scope("section_average"):
        back, mean = call(
            reduce_kernel, [VM] * 3, [((devices, 1, 6 * LANES), F32), ((PER, ROWS, LANES), F32)],
            [pltpu.VMEM((devices, LANES), F32)],
        )(got, chunk, table)
    returned = lax.all_to_all(back, "scen", 0, 0, tiled=True)
    with jax.named_scope("selected"):
        early, late, second, pushed_first, pushed_next = call(
            select_kernel, [VM] * 4,
            [(slab, F32), (slab, F32), (field, F32), (slab, F32), (slab, F32)],
        )(returned, kept, table, chunk)
    new_before = shifted(late, "per", 1)
    with jax.named_scope("push_first"):
        (first,) = call(
            push_first_kernel, [VM] * 5 + [FAR] * 2, [((RB + RB // ROWS, ROWS, TILE), F32)],
            scratch(ROWS, 1) + code_scratch, 6, work=heavy // 2,
        )(pushed_first, high, low, carry, table, *codes)
    far = shifted(first, "per", -1)
    late, first = lax.optimization_barrier((late, first))
    pulled_rows = (RB * ROWS, TILE)

    def pulled_of(period, previous, images):
        return call(
            functools.partial(net_kernel, period), [VM] * 7 + [FAR] * 2,
            [(slab, F32), (pulled_rows, F32)], scratch(ROWS, 1) + code_scratch, 6, work=heavy // 2,
        )(previous, images, mean, carry, high, low, table, *codes)

    def primal_of(period, new, pulled, following):
        return call(
            functools.partial(primal_kernel, period), [VM] * 8, [(slab, F32), (slab, F32)],
        )(new, pulled, second, following, mean, upper, carry, table)

    with jax.named_scope("late_period"):
        (images,) = call(
            push_late_kernel, [VM] * 3 + [FAR] * 2, [(slab, F32)],
            scratch(ROWS, 1) + code_scratch, 6, work=heavy // 2,
        )(late, high, low, *codes)
        late_net, pulled = pulled_of(1, early, images)
        far, pulled = lax.optimization_barrier((far, pulled))
        late_new, late_probe = primal_of(1, late, pulled, far)
    probe_before = shifted(late_probe, "per", 1)
    early, pushed_next, late_probe = lax.optimization_barrier((early, pushed_next, late_probe))
    with jax.named_scope("early_period"):
        images, near = call(
            push_early_kernel, [VM] * 6 + [FAR] * 2, [(slab, F32), (slab, F32)],
            scratch(ROWS) + code_scratch, 8, work=heavy,
        )(early, pushed_next, high, low, carry, table, *codes)
        early_net, pulled = pulled_of(0, new_before, images)
        early_new, early_probe = primal_of(0, early, pulled, near)
    with jax.named_scope("second_push"):
        primal, partial = call(
            result_kernel, [VM] * 14 + [FAR] * 2, [(dual_start.shape, F32), (dual_start.shape, F32)],
            [pltpu.VMEM(dual_start.shape, F32)] + scratch(ROWS) + code_scratch
            + [pltpu.SemaphoreType.DMA((1,))], 8, [FAR, VM], heavy,
        )(early_probe, late_probe, high, low, dual_start, demand, early_net, late_net, early, late,
          early_new, late_new, carry, table, *codes)
    with jax.named_scope("correction"):
        (dual,) = call(
            correct_kernel, [VM] * 4, [(dual_start.shape, F32)],
            [pltpu.VMEM(dual_start.shape, F32), pltpu.VMEM((ROWS, feature), F32),
             pltpu.SemaphoreType.DMA((ROWS,))], places=[FAR],
        )(partial, probe_before, carry, table)
    return primal, dual


def solution(mesh):
    return jax.shard_map(
        per_device,
        mesh=mesh,
        in_specs=(
            P("scen", "per", None),
            P("scen", "per", None),
            P("per", None),
            P("per", None),
            P("per", None),
            P("scen"),
            P("per"),
            P("per", None, None),
            P("per", None, None),
            P(),
            P(),
            P(),
            P(None, "per"),
        ),
        out_specs=(P("scen", "per", None), P("scen", "per", None)),
        check_vma=False,
    )
```
